32 devices in a mesh: rows: 8 (over y, x, core), rep: 4 (over z).
Axes of the slice: x: 2, y: 2, z: 4, core: 2. Of those that a mesh axis runs over, the one named last changes fastest.
Arguments:
- features: float32 [4096, 256], P(('rows', 'rep')), may hold values from -6 to 6
- weight: float32 [256, 256], replicated, may hold values from -0.375 to 0.375
- cotangent: float32 [4096, 256], P(('rows', 'rep')), may hold values from -6 to 6
- tiles: float32 [8, 4, 8, 2, 128, 128], P('rows', 'rep'), may hold values from -0.125 to 0.125
- tile_count: int32 [8, 4, 8], P('rows', 'rep'), may hold values from 0 to 2, as said below
- tile_block: int32 [8, 4, 8, 2], P('rows', 'rep'), may hold values from 0 to 3, as said below
Outputs:
- hidden: float32 [4096, 256], P(('rows', 'rep'))
- grad_weight: float32 [256, 256], replicated
- grad_features: float32 [4096, 256], P(('rows', 'rep'))
The draws below stay inside these ranges and needn't reach their ends.
Inputs may be any that keep to these rules, and one draw needn't show every extreme that they name: `tile_count`: at the section equal to the row group, every column block holds 2 live tiles. `tile_block`: the blocks named by one section's slots are distinct; slots at or beyond the section's count are ignored.
All inputs are finite; a program needn't handle non-finite values.
Results may differ from the reference program's by a relative error of at most 0.0001.
Values sent between devices are 32-bit elements; how exact they have to be, the bound alone decides.
A program may use at most 128 MiB of HBM per device.

```python
import math
import jax
import jax.numpy as jnp
from jax import lax

F = 256
BLK = 128
TPS = 2
NODES = 4096
N_ROWS = 8
N_REP = 4


def draw_tile_count(key, part):
    key = jax.random.fold_in(key, 11)
    first_key, second_key = jax.random.split(key)
    level = jax.random.randint(first_key, (N_ROWS, 1, 1), 1, 2 * TPS + 1)
    raw = jax.random.randint(second_key, (N_ROWS, N_REP, N_ROWS), 0, level + 1)
    count = jnp.minimum(raw, TPS)
    own = jnp.arange(N_ROWS)[:, None, None] == jnp.arange(N_ROWS)[None, None, :]
    return jnp.where(own, TPS, count).astype(jnp.int32)


def draw_tile_block(key, part):
    key = jax.random.fold_in(key, 23)
    scores = jax.random.randint(key, (N_ROWS, N_REP, N_ROWS, N_REP), 0, 1 << 20) * N_REP + jnp.arange(N_REP)
    order = jnp.argsort(scores, axis=-1, stable=True)[..., :TPS]
    return order.astype(jnp.int32)


def block_levels(rng, extent, shards, smallest, largest):
    factor_of, own = 1.0, jax.random.fold_in(rng, 6)
    for axis_at, blocks in shards:
        steps = jnp.exp(jax.random.uniform(jax.random.fold_in(own, axis_at), (blocks,), jnp.float32, smallest / len(shards), largest / len(shards)))
        factor_of = factor_of * jnp.repeat(steps, extent[axis_at] // blocks).reshape([-1 if axis == axis_at else 1 for axis in range(len(extent))])
    return factor_of


def bell_draw(stream_key, extent, width, reach, pieces=(), held_as=jnp.bfloat16):
    factor_of = block_levels(stream_key, extent, pieces, -0.22, 0.18) if pieces else 1.0
    values = jax.random.normal(stream_key, extent, jnp.float32) * width * factor_of
    return jnp.minimum(jnp.maximum(values, -reach), reach).astype(held_as)


def setup_inputs(seed: int = 0) -> dict:
    key_of = jax.random.split(jax.random.key(seed), 7)
    return {
        "features": bell_draw(key_of[0], (NODES, F), 1.0, 6.0, ((0, 32),), jnp.float32),
        "weight": bell_draw(key_of[1], (F, F), F ** -0.5, 0.375, (), jnp.float32),
        "cotangent": bell_draw(key_of[2], (NODES, F), 1.0, 6.0, ((0, 32),), jnp.float32),
        "tiles": bell_draw(key_of[3], (N_ROWS, N_REP, N_ROWS, TPS, BLK, BLK), (BLK * N_ROWS * 2) ** -0.5, 0.125, ((0, 8), (1, 4)), jnp.float32),
        "tile_count": draw_tile_count(jax.random.fold_in(key_of[6], 71), 0),
        "tile_block": draw_tile_block(jax.random.fold_in(key_of[6], 71), 0),
    }


def silu_slope(pre):
    sig = jax.nn.sigmoid(pre)
    return sig * (1.0 + pre * (1.0 - sig))

def reference(features, weight, cotangent, tiles, tile_count, tile_block):
    highest = lax.Precision.HIGHEST
    blocks = jnp.arange(N_REP, dtype=jnp.int32)
    slots = jnp.arange(TPS, dtype=jnp.int32)
    select = ((tile_block[..., None] == blocks) & (slots[:, None] < tile_count[..., None, None])).astype(jnp.float32)
    panels = features.reshape(N_ROWS, N_REP, BLK, F)

    def forward_group(pair):
        group_tiles, group_select = pair
        prods = jnp.einsum('rstab,srbf->rstaf', group_tiles, panels, precision=highest)
        return jnp.einsum('rstk,rstaf->kaf', group_select, prods, precision=highest)
    aggregated = lax.map(forward_group, (tiles, select)).reshape(NODES, F)
    pre = jnp.dot(aggregated, weight, precision=highest)
    hidden = jax.nn.silu(pre)
    delta = cotangent * silu_slope(pre)
    grad_weight = jnp.dot(aggregated.T, delta, precision=highest) / math.sqrt(NODES)
    back = jnp.dot(delta, weight.T, precision=highest).reshape(N_ROWS, N_REP, BLK, F)

    def backward_group(carry, triple):
        group_tiles, group_select, group_back = triple
        picked = jnp.einsum('rstk,kaf->rstaf', group_select, group_back, precision=highest)
        return (carry + jnp.einsum('rstab,rstaf->srbf', group_tiles, picked, precision=highest), None)
    start_grad = jnp.zeros((N_ROWS, N_REP, BLK, F), jnp.float32)
    grad_features, _ = lax.scan(backward_group, start_grad, (tiles, select, back))
    return (hidden, grad_weight, grad_features.reshape(NODES, F))
```

```python
import functools
import math

import jax
import jax.numpy as jnp
from jax import lax
from jax.experimental import pallas as pl
from jax.experimental.pallas import tpu as pltpu
from jax.sharding import PartitionSpec as P

MESH = pl.DeviceIdType.MESH
F32 = jnp.float32
BF16 = jnp.bfloat16


def split(x):
    hi = x.astype(BF16)
    return hi, (x - hi.astype(F32)).astype(BF16)


def mm(a, b, dims=((1,), (0,))):
    return lax.dot_general(a, b, (dims, ((), ())), preferred_element_type=F32)


def mm3(a, b, dims=((1,), (0,))):
    (ah, al), (bh, bl) = split(a), split(b)
    return mm(ah, bh, dims) + (mm(ah, bl, dims) + mm(al, bh, dims))


def kernel(feat, weight, cot, tiles, cnt, blks, hid_o, gw_o, gf_o,
           G, T, W, C, Ahi, Alo, AThi, ATlo, Pb, Rb, Bk, Rs, Es, Ec, Er, Ho, Fo,
           wt, ws, wc, wr, wz, wzr, gw,
           loc_sem, a_s, a_r, b_s, b_r, d_s, d_r, e_s, e_r, g_s, g_r):
    blk = T.shape[2]
    secs = T.shape[0]
    reps = Pb.shape[1]
    chips = secs // 2
    quarter = reps * blk
    row = lax.axis_index("rows")
    z = lax.axis_index("rep")
    c = row % 2
    q = row // 2
    x = q % 2
    y = q // 2
    sib = row + 1 - 2 * c
    xn = row + 2 - 4 * x
    yn = row + 4 - 8 * y
    dg = xn + yn - row
    plane = (xn, yn, dg)
    zs = [(z + d) % reps for d in range(1, reps)]

    barrier = pltpu.get_barrier_semaphore()
    peers = [(sib, z)] + [(p, z) for p in plane] + [(row, k) for k in zs]
    for dev in peers:
        pl.semaphore_signal(barrier, inc=1, device_id=dev, device_id_type=MESH)
    loads = [pltpu.make_async_copy(feat.at[:, h * blk:(h + 1) * blk], G.at[h, row], loc_sem.at[h]) for h in range(2)]
    loads += [pltpu.make_async_copy(tiles.at[0, 0], T, loc_sem.at[2]),
              pltpu.make_async_copy(weight, W, loc_sem.at[3]),
              pltpu.make_async_copy(cot, C, loc_sem.at[4])]
    for ld in loads:
        ld.start()
    pl.semaphore_wait(barrier, len(peers))

    sent = []

    def send(src, dst, ss, rs, dev):
        cp = pltpu.make_async_remote_copy(src_ref=src, dst_ref=dst, send_sem=ss, recv_sem=rs,
                                          device_id=dev, device_id_type=MESH)
        cp.start()
        sent.append(cp)
        return cp

    a_cp = []
    for h in range(2):
        loads[h].wait()
        mine = G.at[h, row]
        a_cp.append([send(mine, mine, a_s.at[h, i], a_r.at[h, i], (p, z)) for i, p in enumerate((xn, yn, dg, sib))])

    loads[2].wait()

    def masks(s, k):
        n = cnt[0, 0, s]
        return [jnp.where((blks[0, 0, s, t] == k) & (t < n), 1.0, 0.0).astype(F32) for t in range(T.shape[1])]

    @pl.loop(0, secs)
    def _(s):
        for k in range(reps):
            m = masks(s, k)
            val = T[s, 0] * m[0]
            for t in range(1, T.shape[1]):
                val = val + T[s, t] * m[t]
            hi, lo = split(val)
            cols = pl.ds(pl.multiple_of(s * blk, blk), blk)
            Ahi[k * blk:(k + 1) * blk, cols] = hi
            Alo[k * blk:(k + 1) * blk, cols] = lo

    b_cp = []
    for h in range(2):
        fwd = []
        for i, p in enumerate(plane):
            a_cp[h][i].wait_recv()
            fwd.append(send(G.at[h, p], G.at[h, p], a_s.at[h, 4 + i], a_r.at[h, 4 + i], (sib, z)))
        a_cp[h][3].wait_recv()
        for cp in fwd:
            cp.wait_recv()
        fh, fl = split(G[h].reshape(secs * blk, blk))
        rhs = jnp.concatenate([fh, fl], axis=1)
        acc = mm(Ahi[...], rhs)
        acc = acc[:, :blk] + (acc[:, blk:] + mm(Alo[...], fh))
        Pb[h] = acc.reshape(reps, blk, blk)
        b_cp.append([send(Pb.at[h, k], Rb.at[h, i], b_s.at[h, i], b_r.at[h, i], (row, k)) for i, k in enumerate(zs)])

    @pl.loop(0, secs)
    def _(s):
        tt = [T[s, t].T for t in range(T.shape[1])]
        rows = pl.ds(pl.multiple_of(((s % 2) * chips + s // 2) * blk, blk), blk)
        for k in range(reps):
            m = masks(s, k)
            val = tt[0] * m[0]
            for t in range(1, T.shape[1]):
                val = val + tt[t] * m[t]
            hi, lo = split(val)
            AThi[rows, k * blk:(k + 1) * blk] = hi
            ATlo[rows, k * blk:(k + 1) * blk] = lo

    loads[3].wait()
    loads[4].wait()
    agg = []
    for h in range(2):
        part = Pb[h, z]
        for i in range(reps - 1):
            b_cp[h][i].wait_recv()
            part = part + Rb[h, i]
        agg.append(part)
    agg = jnp.concatenate(agg, axis=1)
    w = W[...]
    pre = mm3(agg, w)
    sig = 1.0 / (1.0 + jnp.exp(-pre))
    delta = C[...] * (sig * (1.0 + pre * (1.0 - sig)))
    back = mm3(delta, w, ((1,), (1,)))
    d_cp = []
    for h in range(2):
        Bk[h, z] = back[:, h * blk:(h + 1) * blk]
        mine = Bk.at[h, z]
        d_cp.append([send(mine, mine, d_s.at[h, i], d_r.at[h, i], (row, k)) for i, k in enumerate(zs)])
    Ho[...] = pre * sig
    hid_cp = pltpu.make_async_copy(Ho, hid_o, loc_sem.at[5])
    hid_cp.start()

    wt[...] = mm3(agg.T, delta) * (1.0 / math.sqrt(blk * secs * reps))
    half = wt.shape[0] // 2
    piece = half // chips
    sub = piece // reps
    oth = pl.multiple_of((1 - c) * half, half)
    own = pl.multiple_of(c * half, half)
    g1 = send(wt.at[pl.ds(oth, half)], ws, g_s.at[0], g_r.at[0], (sib, z))
    g1.wait_recv()
    wc[...] = wt[pl.ds(own, half)] + ws[...]
    g2 = [send(wc.at[pl.ds(pl.multiple_of((p // 2) * piece, piece), piece)], wr.at[i], g_s.at[1 + i], g_r.at[1 + i], (p, z))
          for i, p in enumerate(plane)]

    def rows_start(h):
        for cp in d_cp[h]:
            cp.wait_recv()
        bh, bl = split(Bk[h].reshape(quarter, blk))
        rhs = jnp.concatenate([bh, bl], axis=1)
        out = None
        for first, core in ((True, 1 - c), (False, c)):
            at = pl.ds(pl.multiple_of(core * (chips * blk), chips * blk), chips * blk)
            acc = mm(AThi[at], rhs)
            acc = acc[:, :blk] + (acc[:, blk:] + mm(ATlo[at], bh))
            Rs[h, 0 if first else 1] = acc.reshape(chips, blk, blk)
            if first:
                out = send(Rs.at[h, 0], Es.at[h], e_s.at[h, 0], e_r.at[h, 0], (sib, z))
        return out

    def rows_mid(h, cp):
        cp.wait_recv()
        out = []
        for i, p in enumerate((dg, xn, yn)):
            Ec[h, i] = Rs[h, 1, p // 2] + Es[h, p // 2]
            out.append(send(Ec.at[h, i], Er.at[h, i], e_s.at[h, 1 + i], e_r.at[h, 1 + i], (p, z)))
        return out

    def rows_end(h, cps):
        total = Rs[h, 1, q] + Es[h, q]
        for i, cp in enumerate(cps):
            cp.wait_recv()
            total = total + Er[h, i]
        Fo[:, h * blk:(h + 1) * blk] = total

    e0 = rows_start(0)
    e0 = rows_mid(0, e0)

    at = pl.multiple_of(q * piece, piece)
    total = wc[pl.ds(at, piece)]
    for i in range(3):
        g2[i].wait_recv()
        total = total + wr[i]
    wz[...] = total
    g3 = [send(wz.at[pl.ds(pl.multiple_of(k * sub, sub), sub)], wzr.at[i], g_s.at[4 + i], g_r.at[4 + i], (row, k))
          for i, k in enumerate(zs)]

    e1 = rows_start(1)
    e1 = rows_mid(1, e1)

    total = wz[pl.ds(pl.multiple_of(z * sub, sub), sub)]
    for i in range(reps - 1):
        g3[i].wait_recv()
        total = total + wzr[i]
    top = c * half + q * piece
    mine = pl.ds(pl.multiple_of(top + z * sub, sub), sub)
    gw[mine] = total
    g4 = [send(gw.at[mine], gw.at[mine], g_s.at[7 + i], g_r.at[7 + i], (row, k)) for i, k in enumerate(zs)]
    for cp in g4:
        cp.wait_recv()
    mine = pl.ds(pl.multiple_of(top, piece), piece)
    g5 = [send(gw.at[mine], gw.at[mine], g_s.at[10 + i], g_r.at[10 + i], (p, z)) for i, p in enumerate(plane)]

    rows_end(0, e0)

    for cp in g5:
        cp.wait_recv()
    mine = pl.ds(own, half)
    g6 = send(gw.at[mine], gw.at[mine], g_s.at[13], g_r.at[13], (sib, z))

    rows_end(1, e1)
    f_cp = pltpu.make_async_copy(Fo, gf_o, loc_sem.at[6])
    f_cp.start()
    g6.wait_recv()
    g_cp = pltpu.make_async_copy(gw, gw_o, loc_sem.at[7])
    g_cp.start()
    for cp in sent:
        cp.wait_send()
    hid_cp.wait()
    f_cp.wait()
    g_cp.wait()


def fused(features, weight, cotangent, tiles, tile_count, tile_block):
    blk, width = features.shape
    secs, slots = tiles.shape[2], tiles.shape[3]
    reps = lax.axis_size("rep")
    chips = secs // 2
    half = width // 2
    piece = half // chips
    sub = piece // reps
    V = pltpu.VMEM
    dma = pltpu.SemaphoreType.DMA
    hbm = pl.BlockSpec(memory_space=pl.ANY)
    smem = pl.BlockSpec(memory_space=pltpu.SMEM)
    flops = 2 * 3 * 2 * (reps * blk) * (secs * blk) * width
    return pl.pallas_call(
        kernel,
        out_shape=(jax.ShapeDtypeStruct((blk, width), F32), jax.ShapeDtypeStruct((width, width), F32),
                   jax.ShapeDtypeStruct((blk, width), F32)),
        in_specs=[hbm, hbm, hbm, hbm, smem, smem],
        out_specs=(hbm, hbm, hbm),
        scratch_shapes=[
            V((2, secs, blk, blk), F32), V((secs, slots, blk, blk), F32), V((width, width), F32), V((blk, width), F32),
            V((reps * blk, secs * blk), BF16), V((reps * blk, secs * blk), BF16),
            V((secs * blk, reps * blk), BF16), V((secs * blk, reps * blk), BF16),
            V((2, reps, blk, blk), F32), V((2, reps - 1, blk, blk), F32), V((2, reps, blk, blk), F32),
            V((2, 2, chips, blk, blk), F32), V((2, chips, blk, blk), F32), V((2, 3, blk, blk), F32), V((2, 3, blk, blk), F32),
            V((blk, width), F32), V((blk, width), F32),
            V((width, width), F32), V((half, width), F32), V((half, width), F32), V((3, piece, width), F32),
            V((piece, width), F32), V((reps - 1, sub, width), F32), V((width, width), F32),
            dma((8,)), dma((2, 7)), dma((2, 7)), dma((2, 3)), dma((2, 3)), dma((2, 3)), dma((2, 3)),
            dma((2, 4)), dma((2, 4)), dma((14,)), dma((14,)),
        ],
        compiler_params=pltpu.CompilerParams(collective_id=0, has_side_effects=True, vmem_limit_bytes=48 * 1024 * 1024),
        cost_estimate=pl.CostEstimate(flops=flops, bytes_accessed=4 * tiles.size, transcendentals=blk * width),
        name="graph_step",
    )(features, weight, cotangent, tiles, tile_count, tile_block)


def silu_slope(pre):
    sig = jax.nn.sigmoid(pre)
    return sig * (1.0 + pre * (1.0 - sig))


def body(features, weight, cotangent, tiles, tile_count, tile_block):
    highest = lax.Precision.HIGHEST
    tile_set = tiles[0, 0]
    counts = tile_count[0, 0]
    block_ids = tile_block[0, 0]
    sections = tile_set.shape[0]
    slots = tile_set.shape[1]
    blk = tile_set.shape[2]
    width = features.shape[1]
    groups = lax.axis_size("rep")
    select = (
        (block_ids[..., None] == jnp.arange(groups, dtype=jnp.int32))
        & (jnp.arange(slots, dtype=jnp.int32)[:, None] < counts[:, None, None])
    ).astype(jnp.float32)
    gathered = lax.all_gather(features, "rows", axis=0, tiled=True).reshape(sections, blk, width)
    prods = jnp.einsum("stab,sbf->staf", tile_set, gathered, precision=highest)
    total = jnp.einsum("stk,staf->kaf", select, prods, precision=highest)
    aggregated = lax.psum_scatter(
        total.reshape(groups * blk, width), "rep", scatter_dimension=0, tiled=True
    )
    pre = jnp.dot(aggregated, weight, precision=highest)
    hidden = jax.nn.silu(pre)
    delta = cotangent * silu_slope(pre)
    weight_term = jnp.dot(aggregated.T, delta, precision=highest)
    node_total = blk * lax.axis_size("rows") * groups
    grad_weight = lax.psum(weight_term, ("rows", "rep")) / math.sqrt(node_total)
    back = jnp.dot(delta, weight.T, precision=highest)
    group_back = lax.all_gather(back, "rep", axis=0, tiled=True).reshape(groups, blk, width)
    count = sections * blk
    picked = jnp.einsum("stk,kaf->staf", select, group_back, precision=highest)
    result = jnp.einsum("stab,staf->sbf", tile_set, picked, precision=highest)
    all_terms = result.reshape(count, width)
    grad_features = lax.psum_scatter(all_terms, "rows", scatter_dimension=0, tiled=True)
    return (hidden, grad_weight, grad_features)


def solution(mesh):
    in_specs = (
        P(("rows", "rep"), None),
        P(),
        P(("rows", "rep"), None),
        P("rows", "rep", None, None, None, None),
        P("rows", "rep", None),
        P("rows", "rep", None, None),
    )
    out_specs = (P(("rows", "rep"), None), P(), P(("rows", "rep"), None))
    fits = mesh.shape["rows"] == 8 and mesh.shape["rep"] == 4
    return jax.shard_map(fused if fits else body, mesh=mesh, in_specs=in_specs, out_specs=out_specs, check_vma=False)
```

```python
import functools
import math

import jax
import jax.numpy as jnp
from jax import lax
from jax.experimental import pallas as pl
from jax.experimental.pallas import tpu as pltpu
from jax.sharding import PartitionSpec as P

LIMIT = 60 * 1024 * 1024
MESH = pl.DeviceIdType.MESH
F32 = jnp.float32
BF16 = jnp.bfloat16


def split(x):
    hi = x.astype(BF16)
    return hi, (x - hi.astype(F32)).astype(BF16)


def mm(a, b, dims=((1,), (0,))):
    return lax.dot_general(a, b, (dims, ((), ())), preferred_element_type=F32)


def mm3(a, b, dims=((1,), (0,))):
    (ah, al), (bh, bl) = split(a), split(b)
    return mm(ah, bh, dims) + (mm(ah, bl, dims) + mm(al, bh, dims))


def kernel(feat, weight, cot, tiles, cnt, blks, hid_o, gw_o, gf_o,
           G, T, W, C, Ahi, Alo, AThi, ATlo, Pb, Rb, St, Bk, Rs, Es, Ec, Er, Ho, Fo,
           wt, ws, wc, wr, wz, wzr, gw,
           loc_sem, a_s, a_r, b_s, b_r, st_r, d_s, d_r, e_s, e_r, g_s, g_r):
    blk = T.shape[2]
    secs = T.shape[0]
    reps = Pb.shape[1]
    chips = secs // 2
    quarter = reps * blk
    row = lax.axis_index("rows")
    z = lax.axis_index("rep")
    c = row % 2
    q = row // 2
    x = q % 2
    y = q // 2
    sib = row + 1 - 2 * c
    xn = row + 2 - 4 * x
    yn = row + 4 - 8 * y
    dg = xn + yn - row
    plane = (xn, yn, dg)
    zs = [(z + d) % reps for d in range(1, reps)]
    near = z + 1 - 2 * (z % 2)
    far = (z + 2) % reps
    mir = reps - 1 - z
    inner = (z == 1) | (z == 2)
    outer = (z == 0) | (z == 3)

    barrier = pltpu.get_barrier_semaphore()
    peers = [(sib, z)] + [(p, z) for p in plane] + [(row, k) for k in zs]
    for dev in peers:
        pl.semaphore_signal(barrier, inc=1, device_id=dev, device_id_type=MESH)
    loads = [pltpu.make_async_copy(feat.at[:, h * blk:(h + 1) * blk], G.at[h, row], loc_sem.at[h]) for h in range(2)]
    loads += [pltpu.make_async_copy(tiles.at[0, 0], T, loc_sem.at[2]),
              pltpu.make_async_copy(weight, W, loc_sem.at[3]),
              pltpu.make_async_copy(cot, C, loc_sem.at[4])]
    for ld in loads:
        ld.start()
    pl.semaphore_wait(barrier, len(peers))

    sent = []

    def put(src, dst, ss, rs, dev):
        return pltpu.make_async_remote_copy(src_ref=src, dst_ref=dst, send_sem=ss, recv_sem=rs,
                                            device_id=dev, device_id_type=MESH)

    def send(src, dst, ss, rs, dev):
        cp = pltpu.make_async_remote_copy(src_ref=src, dst_ref=dst, send_sem=ss, recv_sem=rs,
                                          device_id=dev, device_id_type=MESH)
        cp.start()
        sent.append(cp)
        return cp

    a_cp = []
    for h in range(2):
        loads[h].wait()
        mine = G.at[h, row]
        a_cp.append([send(mine, mine, a_s.at[h, i], a_r.at[h, i], (p, z)) for i, p in enumerate((xn, yn, dg, sib))])

    loads[2].wait()

    def masks(s, k):
        n = cnt[0, 0, s]
        return [jnp.where((blks[0, 0, s, t] == k) & (t < n), 1.0, 0.0).astype(F32) for t in range(T.shape[1])]

    @pl.loop(0, secs)
    def _(s):
        for k in range(reps):
            m = masks(s, k)
            val = T[s, 0] * m[0]
            for t in range(1, T.shape[1]):
                val = val + T[s, t] * m[t]
            hi, lo = split(val)
            cols = pl.ds(pl.multiple_of(s * blk, blk), blk)
            Ahi[k * blk:(k + 1) * blk, cols] = hi
            Alo[k * blk:(k + 1) * blk, cols] = lo

    def b_put(h, k, slot, dev):
        return put(Pb.at[h, k], Rb.at[h, slot], b_s.at[h, slot], b_r.at[h, slot], (row, dev))

    def stage_put(h):
        return put(Pb.at[h, mir], St.at[h], b_s.at[h, 2], st_r.at[h], (row, near))

    def combine(h):
        @pl.when(inner)
        def _():
            stage_put(h).wait_recv()
            Pb[h, far] = Pb[h, far] + St[h]
            b_put(h, far, 1, far).start()

    for h in range(2):
        fwd = []
        for i, p in enumerate(plane):
            a_cp[h][i].wait_recv()
            fwd.append(send(G.at[h, p], G.at[h, p], a_s.at[h, 4 + i], a_r.at[h, 4 + i], (sib, z)))
        a_cp[h][3].wait_recv()
        if h == 1:
            combine(0)
        for cp in fwd:
            cp.wait_recv()
        fh, fl = split(G[h].reshape(secs * blk, blk))
        rhs = jnp.concatenate([fh, fl], axis=1)
        acc = mm(Ahi[...], rhs)
        acc = acc[:, :blk] + (acc[:, blk:] + mm(Alo[...], fh))
        Pb[h] = acc.reshape(reps, blk, blk)

        @pl.when(outer)
        def _():
            stage_put(h).start()
            b_put(h, far, 1, far).start()
            b_put(h, near, 0, near).start()

        @pl.when(inner)
        def _():
            b_put(h, mir, 2, mir).start()
            b_put(h, near, 0, near).start()

    @pl.loop(0, secs)
    def _(s):
        tt = [T[s, t].T for t in range(T.shape[1])]
        rows = pl.ds(pl.multiple_of(((s % 2) * chips + s // 2) * blk, blk), blk)
        for k in range(reps):
            m = masks(s, k)
            val = tt[0] * m[0]
            for t in range(1, T.shape[1]):
                val = val + tt[t] * m[t]
            hi, lo = split(val)
            AThi[rows, k * blk:(k + 1) * blk] = hi
            ATlo[rows, k * blk:(k + 1) * blk] = lo

    combine(1)
    loads[3].wait()
    loads[4].wait()
    agg = []
    for h in range(2):
        b_put(h, near, 0, near).wait_recv()
        part = Pb[h, z] + Rb[h, 0]

        @pl.when(inner)
        def _():
            b_put(h, mir, 2, mir).wait_recv()

        @pl.when(outer)
        def _():
            Rb[h, 2] = jnp.zeros_like(Rb[h, 2])

        part = part + Rb[h, 2]
        b_put(h, far, 1, far).wait_recv()
        agg.append(part + Rb[h, 1])
    agg = jnp.concatenate(agg, axis=1)
    w = W[...]
    pre = mm3(agg, w)
    sig = 1.0 / (1.0 + jnp.exp(-pre))
    delta = C[...] * (sig * (1.0 + pre * (1.0 - sig)))
    back = mm3(delta, w, ((1,), (1,)))

    def d_put(h, k, slot, dev):
        return put(Bk.at[h, k], Bk.at[h, k], d_s.at[h, slot], d_r.at[h, slot], (row, dev))

    for h in range(2):
        Bk[h, z] = back[:, h * blk:(h + 1) * blk]
        d_put(h, z, 2, mir).start()

        @pl.when(outer)
        def _():
            d_put(h, z, 1, far).start()

        d_put(h, z, 0, near).start()

    def relay(h):
        @pl.when(inner)
        def _():
            d_put(h, mir, 2, mir).wait_recv()
            d_put(h, mir, 1, near).start()

    Ho[...] = pre * sig
    hid_cp = pltpu.make_async_copy(Ho, hid_o, loc_sem.at[5])
    hid_cp.start()

    relay(0)

    wt[...] = mm3(agg.T, delta) * (1.0 / math.sqrt(blk * secs * reps))
    half = wt.shape[0] // 2
    piece = half // chips
    sub = piece // reps
    oth = pl.multiple_of((1 - c) * half, half)
    own = pl.multiple_of(c * half, half)
    g1 = send(wt.at[pl.ds(oth, half)], ws, g_s.at[0], g_r.at[0], (sib, z))
    g1.wait_recv()
    wc[...] = wt[pl.ds(own, half)] + ws[...]
    g2 = [send(wc.at[pl.ds(pl.multiple_of((p // 2) * piece, piece), piece)], wr.at[i], g_s.at[1 + i], g_r.at[1 + i], (p, z))
          for i, p in enumerate(plane)]

    def rows_start(h):
        d_put(h, near, 0, near).wait_recv()
        d_put(h, far, 1, far).wait_recv()

        @pl.when(outer)
        def _():
            d_put(h, mir, 2, mir).wait_recv()

        bh, bl = split(Bk[h].reshape(quarter, blk))
        rhs = jnp.concatenate([bh, bl], axis=1)
        out = None
        for first, core in ((True, 1 - c), (False, c)):
            at = pl.ds(pl.multiple_of(core * (chips * blk), chips * blk), chips * blk)
            acc = mm(AThi[at], rhs)
            acc = acc[:, :blk] + (acc[:, blk:] + mm(ATlo[at], bh))
            Rs[h, 0 if first else 1] = acc.reshape(chips, blk, blk)
            if first:
                out = [send(Rs.at[h, 0, p // 2], Es.at[h, p // 2], e_s.at[h, 3 + i], e_r.at[h, 3 + i], (sib, z))
                       for i, p in enumerate((dg, xn, yn, row))]
        return out

    def rows_mid(h, cps):
        out = []
        for i, p in enumerate((dg, xn, yn)):
            cps[i].wait_recv()
            Ec[h, i] = Rs[h, 1, p // 2] + Es[h, p // 2]
            out.append(send(Ec.at[h, i], Er.at[h, i], e_s.at[h, i], e_r.at[h, i], (p, z)))
        cps[3].wait_recv()
        return out

    def rows_end(h, cps):
        total = Rs[h, 1, q] + Es[h, q]
        for i, cp in enumerate(cps):
            cp.wait_recv()
            total = total + Er[h, i]
        Fo[:, h * blk:(h + 1) * blk] = total

    e0 = rows_start(0)
    relay(1)
    e0 = rows_mid(0, e0)

    at = pl.multiple_of(q * piece, piece)
    total = wc[pl.ds(at, piece)]
    for i in range(3):
        g2[i].wait_recv()
        total = total + wr[i]
    wz[...] = total
    g3 = [send(wz.at[pl.ds(pl.multiple_of(k * sub, sub), sub)], wzr.at[i], g_s.at[4 + i], g_r.at[4 + i], (row, k))
          for i, k in enumerate(zs)]

    e1 = rows_start(1)
    e1 = rows_mid(1, e1)

    total = wz[pl.ds(pl.multiple_of(z * sub, sub), sub)]
    for i in range(reps - 1):
        g3[i].wait_recv()
        total = total + wzr[i]
    top = c * half + q * piece
    mine = pl.ds(pl.multiple_of(top + z * sub, sub), sub)
    gw[mine] = total
    g4 = [send(gw.at[mine], gw.at[mine], g_s.at[7 + i], g_r.at[7 + i], (row, k)) for i, k in enumerate(zs)]
    for cp in g4:
        cp.wait_recv()
    mine = pl.ds(pl.multiple_of(top, piece), piece)
    g5 = [send(gw.at[mine], gw.at[mine], g_s.at[10 + i], g_r.at[10 + i], (p, z)) for i, p in enumerate(plane)]

    rows_end(0, e0)

    for cp in g5:
        cp.wait_recv()
    mine = pl.ds(own, half)
    g6 = send(gw.at[mine], gw.at[mine], g_s.at[13], g_r.at[13], (sib, z))

    rows_end(1, e1)
    f_cp = pltpu.make_async_copy(Fo, gf_o, loc_sem.at[6])
    f_cp.start()
    g6.wait_recv()
    g_cp = pltpu.make_async_copy(gw, gw_o, loc_sem.at[7])
    g_cp.start()
    for cp in sent:
        cp.wait_send()
    for h in range(2):
        for i in range(3):
            b_put(h, z, i, near).wait_send()
            d_put(h, z, i, near).wait_send()
    hid_cp.wait()
    f_cp.wait()
    g_cp.wait()


def store(a, b, c, x, y, z, sem):
    cps = [pltpu.make_async_copy(s, d, sem.at[i]) for i, (s, d) in enumerate(((a, x), (b, y), (c, z)))]
    for cp in cps:
        cp.start()
    for cp in cps:
        cp.wait()


def fused(features, weight, cotangent, tiles, tile_count, tile_block):
    blk, width = features.shape
    secs, slots = tiles.shape[2], tiles.shape[3]
    reps = lax.axis_size("rep")
    chips = secs // 2
    half = width // 2
    piece = half // chips
    sub = piece // reps
    V = pltpu.VMEM
    dma = pltpu.SemaphoreType.DMA
    hbm = pl.BlockSpec(memory_space=pl.ANY)
    smem = pl.BlockSpec(memory_space=pltpu.SMEM)
    flops = 2 * 3 * 2 * (reps * blk) * (secs * blk) * width
    raw = pl.pallas_call(
        kernel,
        out_shape=(jax.ShapeDtypeStruct((blk, width), F32), jax.ShapeDtypeStruct((width, width), F32),
                   jax.ShapeDtypeStruct((blk, width), F32)),
        in_specs=[hbm, hbm, hbm, hbm, smem, smem],
        out_specs=(hbm, hbm, hbm),
        scratch_shapes=[
            V((2, secs, blk, blk), F32), V((secs, slots, blk, blk), F32), V((width, width), F32), V((blk, width), F32),
            V((reps * blk, secs * blk), BF16), V((reps * blk, secs * blk), BF16),
            V((secs * blk, reps * blk), BF16), V((secs * blk, reps * blk), BF16),
            V((2, reps, blk, blk), F32), V((2, reps - 1, blk, blk), F32), V((2, blk, blk), F32), V((2, reps, blk, blk), F32),
            V((2, 2, chips, blk, blk), F32), V((2, chips, blk, blk), F32), V((2, 3, blk, blk), F32), V((2, 3, blk, blk), F32),
            V((blk, width), F32), V((blk, width), F32),
            V((width, width), F32), V((half, width), F32), V((half, width), F32), V((3, piece, width), F32),
            V((piece, width), F32), V((reps - 1, sub, width), F32), V((width, width), F32),
            dma((8,)), dma((2, 7)), dma((2, 7)), dma((2, 3)), dma((2, 3)), dma((2,)), dma((2, 3)), dma((2, 3)),
            dma((2, 7)), dma((2, 7)), dma((14,)), dma((14,)),
        ],
        compiler_params=pltpu.CompilerParams(collective_id=0, has_side_effects=True, vmem_limit_bytes=LIMIT),
        cost_estimate=pl.CostEstimate(flops=flops, bytes_accessed=4 * tiles.size, transcendentals=blk * width),
        name="graph_step",
    )(features, weight, cotangent, tiles, tile_count, tile_block)
    return pl.pallas_call(
        store,
        out_shape=tuple(jax.ShapeDtypeStruct(r.shape, r.dtype) for r in raw),
        in_specs=[hbm] * 3,
        out_specs=(hbm,) * 3,
        scratch_shapes=[dma((3,))],
        compiler_params=pltpu.CompilerParams(vmem_limit_bytes=LIMIT),
        name="store_results",
    )(*raw)


def silu_slope(pre):
    sig = jax.nn.sigmoid(pre)
    return sig * (1.0 + pre * (1.0 - sig))


def body(features, weight, cotangent, tiles, tile_count, tile_block):
    highest = lax.Precision.HIGHEST
    tile_set = tiles[0, 0]
    counts = tile_count[0, 0]
    block_ids = tile_block[0, 0]
    sections = tile_set.shape[0]
    slots = tile_set.shape[1]
    blk = tile_set.shape[2]
    width = features.shape[1]
    groups = lax.axis_size("rep")
    select = (
        (block_ids[..., None] == jnp.arange(groups, dtype=jnp.int32))
        & (jnp.arange(slots, dtype=jnp.int32)[:, None] < counts[:, None, None])
    ).astype(jnp.float32)
    gathered = lax.all_gather(features, "rows", axis=0, tiled=True).reshape(sections, blk, width)
    prods = jnp.einsum("stab,sbf->staf", tile_set, gathered, precision=highest)
    total = jnp.einsum("stk,staf->kaf", select, prods, precision=highest)
    aggregated = lax.psum_scatter(
        total.reshape(groups * blk, width), "rep", scatter_dimension=0, tiled=True
    )
    pre = jnp.dot(aggregated, weight, precision=highest)
    hidden = jax.nn.silu(pre)
    delta = cotangent * silu_slope(pre)
    weight_term = jnp.dot(aggregated.T, delta, precision=highest)
    node_total = blk * lax.axis_size("rows") * groups
    grad_weight = lax.psum(weight_term, ("rows", "rep")) / math.sqrt(node_total)
    back = jnp.dot(delta, weight.T, precision=highest)
    group_back = lax.all_gather(back, "rep", axis=0, tiled=True).reshape(groups, blk, width)
    count = sections * blk
    picked = jnp.einsum("stk,kaf->staf", select, group_back, precision=highest)
    result = jnp.einsum("stab,staf->sbf", tile_set, picked, precision=highest)
    all_terms = result.reshape(count, width)
    grad_features = lax.psum_scatter(all_terms, "rows", scatter_dimension=0, tiled=True)
    return (hidden, grad_weight, grad_features)


def solution(mesh):
    in_specs = (
        P(("rows", "rep"), None),
        P(),
        P(("rows", "rep"), None),
        P("rows", "rep", None, None, None, None),
        P("rows", "rep", None),
        P("rows", "rep", None, None),
    )
    out_specs = (P(("rows", "rep"), None), P(), P(("rows", "rep"), None))
    fits = mesh.shape["rows"] == 8 and mesh.shape["rep"] == 4
    return jax.shard_map(fused if fits else body, mesh=mesh, in_specs=in_specs, out_specs=out_specs, check_vma=False)
```

```python
import functools
import math

import jax
import jax.numpy as jnp
from jax import lax
from jax.experimental import pallas as pl
from jax.experimental.pallas import tpu as pltpu
from jax.sharding import PartitionSpec as P

LIMIT = 60 * 1024 * 1024
MESH = pl.DeviceIdType.MESH
F32 = jnp.float32
BF16 = jnp.bfloat16


def split(x):
    hi = x.astype(BF16)
    return hi, (x - hi.astype(F32)).astype(BF16)


def mm(a, b, dims=((1,), (0,))):
    return lax.dot_general(a, b, (dims, ((), ())), preferred_element_type=F32)


def mm3(a, b, dims=((1,), (0,))):
    (ah, al), (bh, bl) = split(a), split(b)
    return mm(ah, bh, dims) + (mm(ah, bl, dims) + mm(al, bh, dims))


def kernel(feat, weight, cot, tiles, cnt, blks, hid_o, gw_o, gf_o,
           G, T, W, C, Ahi, Alo, AThi, ATlo, Pb, Rb, St, Bk, Rs, Es, Ec, Er, Ho, Fo,
           wt, ws, wc, wr, wz, wzr, gw,
           loc_sem, a_s, a_r, b_s, b_r, st_r, d_s, d_r, e_s, e_r, g_s, g_r):
    blk = T.shape[2]
    secs = T.shape[0]
    reps = Pb.shape[1]
    chips = secs // 2
    quarter = reps * blk
    row = lax.axis_index("rows")
    z = lax.axis_index("rep")
    c = row % 2
    q = row // 2
    x = q % 2
    y = q // 2
    sib = row + 1 - 2 * c
    xn = row + 2 - 4 * x
    yn = row + 4 - 8 * y
    dg = xn + yn - row
    plane = (dg, xn, yn)
    zs = [(z + d) % reps for d in range(1, reps)]
    near = z + 1 - 2 * (z % 2)
    far = (z + 2) % reps
    mir = reps - 1 - z
    inner = (z == 1) | (z == 2)
    outer = (z == 0) | (z == 3)

    barrier = pltpu.get_barrier_semaphore()
    peers = [(sib, z)] + [(p, z) for p in plane] + [(row, k) for k in zs]
    for dev in peers:
        pl.semaphore_signal(barrier, inc=1, device_id=dev, device_id_type=MESH)
    loads = [pltpu.make_async_copy(feat.at[:, h * blk:(h + 1) * blk], G.at[h, row], loc_sem.at[h]) for h in range(2)]
    loads += [pltpu.make_async_copy(tiles.at[0, 0], T, loc_sem.at[2]),
              pltpu.make_async_copy(weight, W, loc_sem.at[3]),
              pltpu.make_async_copy(cot, C, loc_sem.at[4])]
    for ld in loads:
        ld.start()
    pl.semaphore_wait(barrier, len(peers))

    sent = []

    def put(src, dst, ss, rs, dev):
        return pltpu.make_async_remote_copy(src_ref=src, dst_ref=dst, send_sem=ss, recv_sem=rs,
                                            device_id=dev, device_id_type=MESH)

    def send(src, dst, ss, rs, dev):
        cp = pltpu.make_async_remote_copy(src_ref=src, dst_ref=dst, send_sem=ss, recv_sem=rs,
                                          device_id=dev, device_id_type=MESH)
        cp.start()
        sent.append(cp)
        return cp

    a_cp = []

    def gather(h):
        loads[h].wait()
        mine = G.at[h, row]
        a_cp.append([send(mine, mine, a_s.at[h, i], a_r.at[h, i], (p, z)) for i, p in enumerate((dg, xn, yn, sib))])

    gather(0)

    loads[2].wait()

    def masks(s, k):
        n = cnt[0, 0, s]
        return [jnp.where((blks[0, 0, s, t] == k) & (t < n), 1.0, 0.0).astype(F32) for t in range(T.shape[1])]

    @pl.loop(0, secs)
    def _(s):
        for k in range(reps):
            m = masks(s, k)
            val = T[s, 0] * m[0]
            for t in range(1, T.shape[1]):
                val = val + T[s, t] * m[t]
            hi, lo = split(val)
            cols = pl.ds(pl.multiple_of(s * blk, blk), blk)
            Ahi[k * blk:(k + 1) * blk, cols] = hi
            Alo[k * blk:(k + 1) * blk, cols] = lo

    rh = blk // 2
    b_pc = ((0, 0, blk), (1, 0, rh), (1, rh, rh))
    d_pc = ((0, 0, rh), (0, rh, rh), (1, 0, blk))

    def b_put(n, k, slot, dev):
        h, at, size = b_pc[n]
        return put(Pb.at[h, k, at:at + size], Rb.at[h, slot, at:at + size], b_s.at[n, slot], b_r.at[n, slot], (row, dev))

    def stage_put(n):
        h, at, size = b_pc[n]
        return put(Pb.at[h, mir, at:at + size], St.at[h, at:at + size], b_s.at[n, 2], st_r.at[n], (row, near))

    def b_send(n):
        @pl.when(outer)
        def _():
            stage_put(n).start()
            b_put(n, far, 1, far).start()
            b_put(n, near, 0, near).start()

        @pl.when(inner)
        def _():
            b_put(n, mir, 2, mir).start()
            b_put(n, near, 0, near).start()

    def combine(n):
        h, at, size = b_pc[n]

        @pl.when(inner)
        def _():
            stage_put(n).wait_recv()
            Pb[h, far, at:at + size] = Pb[h, far, at:at + size] + St[h, at:at + size]
            b_put(n, far, 1, far).start()

    def b_sum(n):
        h, at, size = b_pc[n]
        b_put(n, near, 0, near).wait_recv()
        part = Pb[h, z, at:at + size] + Rb[h, 0, at:at + size]

        @pl.when(inner)
        def _():
            b_put(n, mir, 2, mir).wait_recv()

        @pl.when(outer)
        def _():
            Rb[h, 2, at:at + size] = jnp.zeros((size, blk), F32)

        part = part + Rb[h, 2, at:at + size]
        b_put(n, far, 1, far).wait_recv()
        return part + Rb[h, 1, at:at + size]

    for h in range(2):
        fwd = []
        for i, p in enumerate(plane):
            a_cp[h][i].wait_recv()
            fwd.append(send(G.at[h, p], G.at[h, p], a_s.at[h, 4 + i], a_r.at[h, 4 + i], (sib, z)))
        a_cp[h][3].wait_recv()
        if h == 0:
            gather(1)
        else:
            combine(0)
        for cp in fwd:
            cp.wait_recv()
        fh, fl = split(G[h].reshape(secs * blk, blk))
        rhs = jnp.concatenate([fh, fl], axis=1)
        acc = mm(Ahi[...], rhs)
        acc = acc[:, :blk] + (acc[:, blk:] + mm(Alo[...], fh))
        Pb[h] = acc.reshape(reps, blk, blk)
        for n in ((0,), (1, 2))[h]:
            b_send(n)

    @pl.loop(0, secs)
    def _(s):
        tt = [T[s, t].T for t in range(T.shape[1])]
        rows = pl.ds(pl.multiple_of(((s % 2) * chips + s // 2) * blk, blk), blk)
        for k in range(reps):
            m = masks(s, k)
            val = tt[0] * m[0]
            for t in range(1, T.shape[1]):
                val = val + tt[t] * m[t]
            hi, lo = split(val)
            AThi[rows, k * blk:(k + 1) * blk] = hi
            ATlo[rows, k * blk:(k + 1) * blk] = lo

    combine(1)
    combine(2)
    loads[3].wait()
    loads[4].wait()

    def d_put(n, k, slot, dev):
        h, at, size = d_pc[n]
        ref = Bk.at[h, k, at:at + size]
        return put(ref, ref, d_s.at[n, slot], d_r.at[n, slot], (row, dev))

    def d_send(n):
        d_put(n, z, 2, mir).start()

        @pl.when(outer)
        def _():
            d_put(n, z, 1, far).start()

        d_put(n, z, 0, near).start()

    w = W[...]
    agg0 = b_sum(0)
    pre0 = mm3(agg0, w[:blk])
    agg1, delta = [], []
    for n in (1, 2):
        at = b_pc[n][1]
        agg1.append(b_sum(n))
        pre = pre0[at:at + rh] + mm3(agg1[-1], w[blk:])
        sig = 1.0 / (1.0 + jnp.exp(-pre))
        delta.append(C[at:at + rh] * (sig * (1.0 + pre * (1.0 - sig))))
        back = mm3(delta[-1], w, ((1,), (1,)))
        for h in range(2):
            Bk[h, z, at:at + rh] = back[:, h * blk:(h + 1) * blk]
        d_send(n - 1)
        Ho[at:at + rh] = pre * sig
    d_send(2)
    agg = jnp.concatenate([agg0, jnp.concatenate(agg1, axis=0)], axis=1)
    delta = jnp.concatenate(delta, axis=0)
    hid_cp = pltpu.make_async_copy(Ho, hid_o, loc_sem.at[5])
    hid_cp.start()

    def relay(n):
        @pl.when(inner)
        def _():
            d_put(n, mir, 2, mir).wait_recv()
            d_put(n, mir, 1, near).start()

    relay(0)
    relay(1)

    wt[...] = mm3(agg.T, delta) * (1.0 / math.sqrt(blk * secs * reps))
    half = wt.shape[0] // 2
    piece = half // chips
    sub = piece // reps
    oth = pl.multiple_of((1 - c) * half, half)
    own = pl.multiple_of(c * half, half)
    g1 = send(wt.at[pl.ds(oth, half)], ws, g_s.at[0], g_r.at[0], (sib, z))
    g1.wait_recv()
    wc[...] = wt[pl.ds(own, half)] + ws[...]
    g2 = [send(wc.at[pl.ds(pl.multiple_of((p // 2) * piece, piece), piece)], wr.at[i], g_s.at[1 + i], g_r.at[1 + i], (p, z))
          for i, p in enumerate(plane)]

    def rows_start(h):
        for n in ((0, 1), (2,))[h]:
            d_put(n, near, 0, near).wait_recv()
            d_put(n, far, 1, far).wait_recv()

        @pl.when(outer)
        def _():
            for n in ((0, 1), (2,))[h]:
                d_put(n, mir, 2, mir).wait_recv()

        bh, bl = split(Bk[h].reshape(quarter, blk))
        rhs = jnp.concatenate([bh, bl], axis=1)
        out = None
        for first, core in ((True, 1 - c), (False, c)):
            at = pl.ds(pl.multiple_of(core * (chips * blk), chips * blk), chips * blk)
            acc = mm(AThi[at], rhs)
            acc = acc[:, :blk] + (acc[:, blk:] + mm(ATlo[at], bh))
            Rs[h, 0 if first else 1] = acc.reshape(chips, blk, blk)
            if first:
                out = [send(Rs.at[h, 0, p // 2], Es.at[h, p // 2], e_s.at[h, 3 + i], e_r.at[h, 3 + i], (sib, z))
                       for i, p in enumerate((dg, xn, yn, row))]
        return out

    def rows_mid(h, cps):
        out = []
        for i, p in enumerate((dg, xn, yn)):
            cps[i].wait_recv()
            Ec[h, i] = Rs[h, 1, p // 2] + Es[h, p // 2]
            out.append(send(Ec.at[h, i], Er.at[h, i], e_s.at[h, i], e_r.at[h, i], (p, z)))
        cps[3].wait_recv()
        return out

    def rows_end(h, cps):
        total = Rs[h, 1, q] + Es[h, q]
        for i, cp in enumerate(cps):
            cp.wait_recv()
            total = total + Er[h, i]
        Fo[:, h * blk:(h + 1) * blk] = total

    e0 = rows_start(0)
    relay(2)
    e0 = rows_mid(0, e0)

    at = pl.multiple_of(q * piece, piece)
    total = wc[pl.ds(at, piece)]
    for i in range(3):
        g2[i].wait_recv()
        total = total + wr[i]
    wz[...] = total
    g3 = [send(wz.at[pl.ds(pl.multiple_of(k * sub, sub), sub)], wzr.at[i], g_s.at[4 + i], g_r.at[4 + i], (row, k))
          for i, k in enumerate(zs)]

    e1 = rows_start(1)
    e1 = rows_mid(1, e1)

    total = wz[pl.ds(pl.multiple_of(z * sub, sub), sub)]
    for i in range(reps - 1):
        g3[i].wait_recv()
        total = total + wzr[i]
    top = c * half + q * piece
    mine = pl.ds(pl.multiple_of(top + z * sub, sub), sub)
    gw[mine] = total
    g4 = [send(gw.at[mine], gw.at[mine], g_s.at[7 + i], g_r.at[7 + i], (row, k)) for i, k in enumerate(zs)]
    for cp in g4:
        cp.wait_recv()
    mine = pl.ds(pl.multiple_of(top, piece), piece)
    g5 = [send(gw.at[mine], gw.at[mine], g_s.at[10 + i], g_r.at[10 + i], (p, z)) for i, p in enumerate(plane)]

    rows_end(0, e0)

    for cp in g5:
        cp.wait_recv()
    mine = pl.ds(own, half)
    g6 = send(gw.at[mine], gw.at[mine], g_s.at[13], g_r.at[13], (sib, z))

    rows_end(1, e1)
    f_cp = pltpu.make_async_copy(Fo, gf_o, loc_sem.at[6])
    f_cp.start()
    g6.wait_recv()
    g_cp = pltpu.make_async_copy(gw, gw_o, loc_sem.at[7])
    g_cp.start()
    for cp in sent:
        cp.wait_send()
    for n in range(3):
        for i in range(3):
            b_put(n, z, i, near).wait_send()
            d_put(n, z, i, near).wait_send()
    hid_cp.wait()
    f_cp.wait()
    g_cp.wait()


def store(a, b, c, x, y, z, u, v, w, sem):
    bufs = ((a, u, x), (b, v, y), (c, w, z))
    ins = [pltpu.make_async_copy(s, t, sem.at[0, i]) for i, (s, t, _) in enumerate(bufs)]
    outs = [pltpu.make_async_copy(t, d, sem.at[1, i]) for i, (_, t, d) in enumerate(bufs)]
    for cp in ins:
        cp.start()
    for cp, out in zip(ins, outs):
        cp.wait()
        out.start()
    for out in outs:
        out.wait()


def fused(features, weight, cotangent, tiles, tile_count, tile_block):
    blk, width = features.shape
    secs, slots = tiles.shape[2], tiles.shape[3]
    reps = lax.axis_size("rep")
    chips = secs // 2
    half = width // 2
    piece = half // chips
    sub = piece // reps
    V = pltpu.VMEM
    dma = pltpu.SemaphoreType.DMA
    hbm = pl.BlockSpec(memory_space=pltpu.HBM)
    smem = pl.BlockSpec(memory_space=pltpu.SMEM)
    flops = 2 * 3 * 2 * (reps * blk) * (secs * blk) * width
    raw = pl.pallas_call(
        kernel,
        out_shape=(jax.ShapeDtypeStruct((blk, width), F32), jax.ShapeDtypeStruct((width, width), F32),
                   jax.ShapeDtypeStruct((blk, width), F32)),
        in_specs=[hbm, hbm, hbm, hbm, smem, smem],
        out_specs=(hbm,) * 3,
        scratch_shapes=[
            V((2, secs, blk, blk), F32), V((secs, slots, blk, blk), F32), V((width, width), F32), V((blk, width), F32),
            V((reps * blk, secs * blk), BF16), V((reps * blk, secs * blk), BF16),
            V((secs * blk, reps * blk), BF16), V((secs * blk, reps * blk), BF16),
            V((2, reps, blk, blk), F32), V((2, reps - 1, blk, blk), F32), V((2, blk, blk), F32), V((2, reps, blk, blk), F32),
            V((2, 2, chips, blk, blk), F32), V((2, chips, blk, blk), F32), V((2, 3, blk, blk), F32), V((2, 3, blk, blk), F32),
            V((blk, width), F32), V((blk, width), F32),
            V((width, width), F32), V((half, width), F32), V((half, width), F32), V((3, piece, width), F32),
            V((piece, width), F32), V((reps - 1, sub, width), F32), V((width, width), F32),
            dma((8,)), dma((2, 7)), dma((2, 7)), dma((3, 3)), dma((3, 3)), dma((3,)), dma((3, 3)), dma((3, 3)),
            dma((2, 7)), dma((2, 7)), dma((14,)), dma((14,)),
        ],
        compiler_params=pltpu.CompilerParams(collective_id=0, has_side_effects=True, vmem_limit_bytes=LIMIT),
        cost_estimate=pl.CostEstimate(flops=flops, bytes_accessed=4 * tiles.size, transcendentals=blk * width),
        name="graph_step",
    )(features, weight, cotangent, tiles, tile_count, tile_block)
    return pl.pallas_call(
        store,
        out_shape=tuple(jax.ShapeDtypeStruct(r.shape, r.dtype) for r in raw),
        in_specs=[hbm] * 3,
        out_specs=(hbm,) * 3,
        scratch_shapes=[V(r.shape, r.dtype) for r in raw] + [dma((2, 3))],
        compiler_params=pltpu.CompilerParams(vmem_limit_bytes=LIMIT),
        name="store_results",
    )(*raw)


def silu_slope(pre):
    sig = jax.nn.sigmoid(pre)
    return sig * (1.0 + pre * (1.0 - sig))


def body(features, weight, cotangent, tiles, tile_count, tile_block):
    highest = lax.Precision.HIGHEST
    tile_set = tiles[0, 0]
    counts = tile_count[0, 0]
    block_ids = tile_block[0, 0]
    sections = tile_set.shape[0]
    slots = tile_set.shape[1]
    blk = tile_set.shape[2]
    width = features.shape[1]
    groups = lax.axis_size("rep")
    select = (
        (block_ids[..., None] == jnp.arange(groups, dtype=jnp.int32))
        & (jnp.arange(slots, dtype=jnp.int32)[:, None] < counts[:, None, None])
    ).astype(jnp.float32)
    gathered = lax.all_gather(features, "rows", axis=0, tiled=True).reshape(sections, blk, width)
    prods = jnp.einsum("stab,sbf->staf", tile_set, gathered, precision=highest)
    total = jnp.einsum("stk,staf->kaf", select, prods, precision=highest)
    aggregated = lax.psum_scatter(
        total.reshape(groups * blk, width), "rep", scatter_dimension=0, tiled=True
    )
    pre = jnp.dot(aggregated, weight, precision=highest)
    hidden = jax.nn.silu(pre)
    delta = cotangent * silu_slope(pre)
    weight_term = jnp.dot(aggregated.T, delta, precision=highest)
    node_total = blk * lax.axis_size("rows") * groups
    grad_weight = lax.psum(weight_term, ("rows", "rep")) / math.sqrt(node_total)
    back = jnp.dot(delta, weight.T, precision=highest)
    group_back = lax.all_gather(back, "rep", axis=0, tiled=True).reshape(groups, blk, width)
    count = sections * blk
    picked = jnp.einsum("stk,kaf->staf", select, group_back, precision=highest)
    result = jnp.einsum("stab,staf->sbf", tile_set, picked, precision=highest)
    all_terms = result.reshape(count, width)
    grad_features = lax.psum_scatter(all_terms, "rows", scatter_dimension=0, tiled=True)
    return (hidden, grad_weight, grad_features)


def solution(mesh):
    in_specs = (
        P(("rows", "rep"), None),
        P(),
        P(("rows", "rep"), None),
        P("rows", "rep", None, None, None, None),
        P("rows", "rep", None),
        P("rows", "rep", None, None),
    )
    out_specs = (P(("rows", "rep"), None), P(), P(("rows", "rep"), None))
    fits = mesh.shape["rows"] == 8 and mesh.shape["rep"] == 4
    return jax.shard_map(fused if fits else body, mesh=mesh, in_specs=in_specs, out_specs=out_specs, check_vma=False)
```

```python
import functools
import math

import jax
import jax.numpy as jnp
from jax import lax
from jax.experimental import pallas as pl
from jax.experimental.pallas import tpu as pltpu
from jax.sharding import PartitionSpec as P

LIMIT = 60 * 1024 * 1024
MESH = pl.DeviceIdType.MESH
F32 = jnp.float32
BF16 = jnp.bfloat16


def split(x):
    hi = x.astype(BF16)
    return hi, (x - hi.astype(F32)).astype(BF16)


def mm(a, b, dims=((1,), (0,))):
    return lax.dot_general(a, b, (dims, ((), ())), preferred_element_type=F32)


def mm3(a, b, dims=((1,), (0,))):
    (ah, al), (bh, bl) = split(a), split(b)
    return mm(ah, bh, dims) + (mm(ah, bl, dims) + mm(al, bh, dims))


def kernel(feat, weight, cot, tiles, cnt, blks, hid_o, gw_o, gf_o,
           G, T, W, C, Ahi, Alo, AThi, ATlo, Pb, Rb, St, Bk, Rs, Es, Ec, Er, Ho, Fo,
           wt, ws, wc, wr, wz, wzr, gw,
           loc_sem, a_s, a_r, b_s, b_r, st_r, d_s, d_r, e_s, e_r, g_s, g_r):
    blk = T.shape[2]
    secs = T.shape[0]
    reps = Pb.shape[1]
    chips = secs // 2
    quarter = reps * blk
    row = lax.axis_index("rows")
    z = lax.axis_index("rep")
    c = row % 2
    q = row // 2
    x = q % 2
    y = q // 2
    sib = row + 1 - 2 * c
    xn = row + 2 - 4 * x
    yn = row + 4 - 8 * y
    dg = xn + yn - row
    plane = (dg, xn, yn)
    zs = [(z + d) % reps for d in range(1, reps)]
    near = z + 1 - 2 * (z % 2)
    far = (z + 2) % reps
    mir = reps - 1 - z
    inner = (z == 1) | (z == 2)
    outer = (z == 0) | (z == 3)

    barrier = pltpu.get_barrier_semaphore()
    peers = [(sib, z)] + [(p, z) for p in plane] + [(row, k) for k in zs]
    for dev in peers:
        pl.semaphore_signal(barrier, inc=1, device_id=dev, device_id_type=MESH)
    loads = [pltpu.make_async_copy(feat.at[:, h * blk:(h + 1) * blk], G.at[h, row], loc_sem.at[h]) for h in range(2)]
    loads += [pltpu.make_async_copy(tiles.at[0, 0], T, loc_sem.at[2]),
              pltpu.make_async_copy(weight, W, loc_sem.at[3]),
              pltpu.make_async_copy(cot, C, loc_sem.at[4])]
    for ld in loads:
        ld.start()
    pl.semaphore_wait(barrier, len(peers))

    sent = []

    def put(src, dst, ss, rs, dev):
        return pltpu.make_async_remote_copy(src_ref=src, dst_ref=dst, send_sem=ss, recv_sem=rs,
                                            device_id=dev, device_id_type=MESH)

    def send(src, dst, ss, rs, dev):
        cp = pltpu.make_async_remote_copy(src_ref=src, dst_ref=dst, send_sem=ss, recv_sem=rs,
                                          device_id=dev, device_id_type=MESH)
        cp.start()
        sent.append(cp)
        return cp

    a_cp = []

    def gather(h):
        loads[h].wait()
        mine = G.at[h, row]
        a_cp.append([send(mine, mine, a_s.at[h, i], a_r.at[h, i], (p, z)) for i, p in enumerate((dg, xn, yn, sib))])

    gather(0)

    loads[2].wait()

    def masks(s, k):
        n = cnt[0, 0, s]
        return [jnp.where((blks[0, 0, t, s] == k) & (t < n), 1.0, 0.0).astype(F32) for t in range(T.shape[1])]

    @pl.loop(0, secs)
    def _(s):
        for k in range(reps):
            m = masks(s, k)
            val = T[s, 0] * m[0]
            for t in range(1, T.shape[1]):
                val = val + T[s, t] * m[t]
            hi, lo = split(val)
            cols = pl.ds(pl.multiple_of(s * blk, blk), blk)
            Ahi[k * blk:(k + 1) * blk, cols] = hi
            Alo[k * blk:(k + 1) * blk, cols] = lo

    rh = blk // 2
    b_pc = ((0, 0, blk), (1, 0, rh), (1, rh, rh))
    d_pc = ((0, 0, rh), (0, rh, rh), (1, 0, blk))

    def b_put(n, k, slot, dev):
        h, at, size = b_pc[n]
        return put(Pb.at[h, k, at:at + size], Rb.at[h, slot, at:at + size], b_s.at[n, slot], b_r.at[n, slot], (row, dev))

    def stage_put(n):
        h, at, size = b_pc[n]
        return put(Pb.at[h, mir, at:at + size], St.at[h, at:at + size], b_s.at[n, 2], st_r.at[n], (row, near))

    def b_send(n):
        @pl.when(outer)
        def _():
            stage_put(n).start()
            b_put(n, far, 1, far).start()
            b_put(n, near, 0, near).start()

        @pl.when(inner)
        def _():
            b_put(n, mir, 2, mir).start()
            b_put(n, near, 0, near).start()

    def combine(n):
        h, at, size = b_pc[n]

        @pl.when(inner)
        def _():
            stage_put(n).wait_recv()
            Pb[h, far, at:at + size] = Pb[h, far, at:at + size] + St[h, at:at + size]
            b_put(n, far, 1, far).start()

    def b_sum(n):
        h, at, size = b_pc[n]
        b_put(n, near, 0, near).wait_recv()
        part = Pb[h, z, at:at + size] + Rb[h, 0, at:at + size]

        @pl.when(inner)
        def _():
            b_put(n, mir, 2, mir).wait_recv()

        @pl.when(outer)
        def _():
            Rb[h, 2, at:at + size] = jnp.zeros((size, blk), F32)

        part = part + Rb[h, 2, at:at + size]
        b_put(n, far, 1, far).wait_recv()
        return part + Rb[h, 1, at:at + size]

    for h in range(2):
        fwd = []
        for i, p in ((1, xn), (2, yn), (0, dg)):
            a_cp[h][i].wait_recv()
            fwd.append(send(G.at[h, p], G.at[h, p], a_s.at[h, 4 + i], a_r.at[h, 4 + i], (sib, z)))
        a_cp[h][3].wait_recv()
        if h == 0:
            gather(1)
        else:
            combine(0)
        for cp in fwd:
            cp.wait_recv()
        fh, fl = split(G[h].reshape(secs * blk, blk))
        rhs = jnp.concatenate([fh, fl], axis=1)
        acc = mm(Ahi[...], rhs)
        acc = acc[:, :blk] + (acc[:, blk:] + mm(Alo[...], fh))
        Pb[h] = acc.reshape(reps, blk, blk)
        for n in ((0,), (1, 2))[h]:
            b_send(n)

    @pl.loop(0, secs)
    def _(s):
        tt = [T[s, t].T for t in range(T.shape[1])]
        rows = pl.ds(pl.multiple_of(((s % 2) * chips + s // 2) * blk, blk), blk)
        for k in range(reps):
            m = masks(s, k)
            val = tt[0] * m[0]
            for t in range(1, T.shape[1]):
                val = val + tt[t] * m[t]
            hi, lo = split(val)
            AThi[rows, k * blk:(k + 1) * blk] = hi
            ATlo[rows, k * blk:(k + 1) * blk] = lo

    combine(1)
    combine(2)
    loads[3].wait()
    loads[4].wait()

    def d_put(n, k, slot, dev):
        h, at, size = d_pc[n]
        ref = Bk.at[h, k, at:at + size]
        return put(ref, ref, d_s.at[n, slot], d_r.at[n, slot], (row, dev))

    def d_send(n):
        d_put(n, z, 2, mir).start()

        @pl.when(outer)
        def _():
            d_put(n, z, 1, far).start()

        d_put(n, z, 0, near).start()

    w = W[...]
    agg0 = b_sum(0)
    pre0 = mm3(agg0, w[:blk])
    agg1, delta = [], []
    for n in (1, 2):
        at = b_pc[n][1]
        agg1.append(b_sum(n))
        pre = pre0[at:at + rh] + mm3(agg1[-1], w[blk:])
        sig = 1.0 / (1.0 + jnp.exp(-pre))
        delta.append(C[at:at + rh] * (sig * (1.0 + pre * (1.0 - sig))))
        back = mm3(delta[-1], w, ((1,), (1,)))
        for h in range(2):
            Bk[h, z, at:at + rh] = back[:, h * blk:(h + 1) * blk]
        d_send(n - 1)
        Ho[at:at + rh] = pre * sig
    d_send(2)
    agg = jnp.concatenate([agg0, jnp.concatenate(agg1, axis=0)], axis=1)
    delta = jnp.concatenate(delta, axis=0)
    hid_cp = pltpu.make_async_copy(Ho, hid_o, loc_sem.at[5])
    hid_cp.start()

    def relay(n):
        @pl.when(inner)
        def _():
            d_put(n, mir, 2, mir).wait_recv()
            d_put(n, mir, 1, near).start()


    wt[...] = mm3(agg.T, delta) * (1.0 / math.sqrt(blk * secs * reps))
    half = wt.shape[0] // 2
    piece = half // chips
    sub = piece // reps
    oth = pl.multiple_of((1 - c) * half, half)
    own = pl.multiple_of(c * half, half)
    g1 = send(wt.at[pl.ds(oth, half)], ws, g_s.at[0], g_r.at[0], (sib, z))
    relay(0)
    relay(1)
    g1.wait_recv()
    wc[...] = wt[pl.ds(own, half)] + ws[...]
    g2 = [send(wc.at[pl.ds(pl.multiple_of((p // 2) * piece, piece), piece)], wr.at[i], g_s.at[1 + i], g_r.at[1 + i], (p, z))
          for i, p in enumerate(plane)]

    def rows_start(h):
        for n in ((0, 1), (2,))[h]:
            d_put(n, near, 0, near).wait_recv()
            d_put(n, far, 1, far).wait_recv()

        @pl.when(outer)
        def _():
            for n in ((0, 1), (2,))[h]:
                d_put(n, mir, 2, mir).wait_recv()

        bh, bl = split(Bk[h].reshape(quarter, blk))
        rhs = jnp.concatenate([bh, bl], axis=1)
        out = None
        for first, core in ((True, 1 - c), (False, c)):
            at = pl.ds(pl.multiple_of(core * (chips * blk), chips * blk), chips * blk)
            acc = mm(AThi[at], rhs)
            acc = acc[:, :blk] + (acc[:, blk:] + mm(ATlo[at], bh))
            Rs[h, 0 if first else 1] = acc.reshape(chips, blk, blk)
            if first:
                out = [send(Rs.at[h, 0, p // 2], Es.at[h, p // 2], e_s.at[h, 3 + i], e_r.at[h, 3 + i], (sib, z))
                       for i, p in enumerate((dg, xn, yn, row))]
        return out

    def rows_mid(h, cps):
        out = []
        for i, p in enumerate((dg, xn, yn)):
            cps[i].wait_recv()
            Ec[h, i] = Rs[h, 1, p // 2] + Es[h, p // 2]
            out.append(send(Ec.at[h, i], Er.at[h, i], e_s.at[h, i], e_r.at[h, i], (p, z)))
        cps[3].wait_recv()
        return out

    def rows_end(h, cps):
        total = Rs[h, 1, q] + Es[h, q]
        for i, cp in enumerate(cps):
            cp.wait_recv()
            total = total + Er[h, i]
        Fo[:, h * blk:(h + 1) * blk] = total

    e0 = rows_start(0)
    relay(2)
    e0 = rows_mid(0, e0)

    at = pl.multiple_of(q * piece, piece)
    total = wc[pl.ds(at, piece)]
    for i in range(3):
        g2[i].wait_recv()
        total = total + wr[i]
    wz[...] = total
    g3 = [send(wz.at[pl.ds(pl.multiple_of(k * sub, sub), sub)], wzr.at[i], g_s.at[4 + i], g_r.at[4 + i], (row, k))
          for i, k in enumerate(zs)]

    total = wz[pl.ds(pl.multiple_of(z * sub, sub), sub)]
    for i in range(reps - 1):
        g3[i].wait_recv()
        total = total + wzr[i]
    top = c * half + q * piece
    mine = pl.ds(pl.multiple_of(top + z * sub, sub), sub)
    gw[mine] = total
    g4 = [send(gw.at[mine], gw.at[mine], g_s.at[7 + i], g_r.at[7 + i], (row, k)) for i, k in enumerate(zs)]
    e1 = rows_start(1)
    for cp in g4:
        cp.wait_recv()
    mine = pl.ds(pl.multiple_of(top, piece), piece)
    g5 = [send(gw.at[mine], gw.at[mine], g_s.at[10 + i], g_r.at[10 + i], (p, z)) for i, p in enumerate(plane)]

    e1 = rows_mid(1, e1)
    rows_end(0, e0)

    for cp in g5:
        cp.wait_recv()
    mine = pl.ds(own, half)
    g6 = send(gw.at[mine], gw.at[mine], g_s.at[13], g_r.at[13], (sib, z))

    rows_end(1, e1)
    f_cp = pltpu.make_async_copy(Fo, gf_o, loc_sem.at[6])
    f_cp.start()
    g6.wait_recv()
    g_cp = pltpu.make_async_copy(gw, gw_o, loc_sem.at[7])
    g_cp.start()
    for cp in sent:
        cp.wait_send()
    for n in range(3):
        for i in range(3):
            b_put(n, z, i, near).wait_send()
            d_put(n, z, i, near).wait_send()
    hid_cp.wait()
    f_cp.wait()
    g_cp.wait()


def store(a, b, c, x, y, z, u, v, w, sem):
    bufs = ((a, u, x), (b, v, y), (c, w, z))
    ins = [pltpu.make_async_copy(s, t, sem.at[0, i]) for i, (s, t, _) in enumerate(bufs)]
    outs = [pltpu.make_async_copy(t, d, sem.at[1, i]) for i, (_, t, d) in enumerate(bufs)]
    for cp in ins:
        cp.start()
    for cp, out in zip(ins, outs):
        cp.wait()
        out.start()
    for out in outs:
        out.wait()


def fused(features, weight, cotangent, tiles, tile_count, tile_block):
    blk, width = features.shape
    secs, slots = tiles.shape[2], tiles.shape[3]
    reps = lax.axis_size("rep")
    chips = secs // 2
    half = width // 2
    piece = half // chips
    sub = piece // reps
    V = pltpu.VMEM
    dma = pltpu.SemaphoreType.DMA
    hbm = pl.BlockSpec(memory_space=pltpu.HBM)
    smem = pl.BlockSpec(memory_space=pltpu.SMEM)
    flops = 2 * 3 * 2 * (reps * blk) * (secs * blk) * width
    raw = pl.pallas_call(
        kernel,
        out_shape=(jax.ShapeDtypeStruct((blk, width), F32), jax.ShapeDtypeStruct((width, width), F32),
                   jax.ShapeDtypeStruct((blk, width), F32)),
        in_specs=[hbm, hbm, hbm, hbm, smem, smem],
        out_specs=(hbm,) * 3,
        scratch_shapes=[
            V((2, secs, blk, blk), F32), V((secs, slots, blk, blk), F32), V((width, width), F32), V((blk, width), F32),
            V((reps * blk, secs * blk), BF16), V((reps * blk, secs * blk), BF16),
            V((secs * blk, reps * blk), BF16), V((secs * blk, reps * blk), BF16),
            V((2, reps, blk, blk), F32), V((2, reps - 1, blk, blk), F32), V((2, blk, blk), F32), V((2, reps, blk, blk), F32),
            V((2, 2, chips, blk, blk), F32), V((2, chips, blk, blk), F32), V((2, 3, blk, blk), F32), V((2, 3, blk, blk), F32),
            V((blk, width), F32), V((blk, width), F32),
            V((width, width), F32), V((half, width), F32), V((half, width), F32), V((3, piece, width), F32),
            V((piece, width), F32), V((reps - 1, sub, width), F32), V((width, width), F32),
            dma((8,)), dma((2, 7)), dma((2, 7)), dma((3, 3)), dma((3, 3)), dma((3,)), dma((3, 3)), dma((3, 3)),
            dma((2, 7)), dma((2, 7)), dma((14,)), dma((14,)),
        ],
        compiler_params=pltpu.CompilerParams(collective_id=0, has_side_effects=True, vmem_limit_bytes=LIMIT),
        cost_estimate=pl.CostEstimate(flops=flops, bytes_accessed=4 * tiles.size, transcendentals=blk * width),
        name="graph_step",
    )(features, weight, cotangent, tiles, tile_count, tile_block.transpose(0, 1, 3, 2))
    return pl.pallas_call(
        store,
        out_shape=tuple(jax.ShapeDtypeStruct(r.shape, r.dtype) for r in raw),
        in_specs=[hbm] * 3,
        out_specs=(hbm,) * 3,
        scratch_shapes=[V(r.shape, r.dtype) for r in raw] + [dma((2, 3))],
        compiler_params=pltpu.CompilerParams(vmem_limit_bytes=LIMIT),
        name="store_results",
    )(*raw)


def silu_slope(pre):
    sig = jax.nn.sigmoid(pre)
    return sig * (1.0 + pre * (1.0 - sig))


def body(features, weight, cotangent, tiles, tile_count, tile_block):
    highest = lax.Precision.HIGHEST
    tile_set = tiles[0, 0]
    counts = tile_count[0, 0]
    block_ids = tile_block[0, 0]
    sections = tile_set.shape[0]
    slots = tile_set.shape[1]
    blk = tile_set.shape[2]
    width = features.shape[1]
    groups = lax.axis_size("rep")
    select = (
        (block_ids[..., None] == jnp.arange(groups, dtype=jnp.int32))
        & (jnp.arange(slots, dtype=jnp.int32)[:, None] < counts[:, None, None])
    ).astype(jnp.float32)
    gathered = lax.all_gather(features, "rows", axis=0, tiled=True).reshape(sections, blk, width)
    prods = jnp.einsum("stab,sbf->staf", tile_set, gathered, precision=highest)
    total = jnp.einsum("stk,staf->kaf", select, prods, precision=highest)
    aggregated = lax.psum_scatter(
        total.reshape(groups * blk, width), "rep", scatter_dimension=0, tiled=True
    )
    pre = jnp.dot(aggregated, weight, precision=highest)
    hidden = jax.nn.silu(pre)
    delta = cotangent * silu_slope(pre)
    weight_term = jnp.dot(aggregated.T, delta, precision=highest)
    node_total = blk * lax.axis_size("rows") * groups
    grad_weight = lax.psum(weight_term, ("rows", "rep")) / math.sqrt(node_total)
    back = jnp.dot(delta, weight.T, precision=highest)
    group_back = lax.all_gather(back, "rep", axis=0, tiled=True).reshape(groups, blk, width)
    count = sections * blk
    picked = jnp.einsum("stk,kaf->staf", select, group_back, precision=highest)
    result = jnp.einsum("stab,staf->sbf", tile_set, picked, precision=highest)
    all_terms = result.reshape(count, width)
    grad_features = lax.psum_scatter(all_terms, "rows", scatter_dimension=0, tiled=True)
    return (hidden, grad_weight, grad_features)


def solution(mesh):
    in_specs = (
        P(("rows", "rep"), None),
        P(),
        P(("rows", "rep"), None),
        P("rows", "rep", None, None, None, None),
        P("rows", "rep", None),
        P("rows", "rep", None, None),
    )
    out_specs = (P(("rows", "rep"), None), P(), P(("rows", "rep"), None))
    fits = mesh.shape["rows"] == 8 and mesh.shape["rep"] == 4
    return jax.shard_map(fused if fits else body, mesh=mesh, in_specs=in_specs, out_specs=out_specs, check_vma=False)
```

```python
import functools
import math

import jax
import jax.numpy as jnp
from jax import lax
from jax.experimental import pallas as pl
from jax.experimental.pallas import tpu as pltpu
from jax.sharding import PartitionSpec as P

LIMIT = 60 * 1024 * 1024
MESH = pl.DeviceIdType.MESH
F32 = jnp.float32
BF16 = jnp.bfloat16


def split(x):
    hi = x.astype(BF16)
    return hi, (x - hi.astype(F32)).astype(BF16)


def mm(a, b, dims=((1,), (0,))):
    return lax.dot_general(a, b, (dims, ((), ())), preferred_element_type=F32)


def mm3(a, b, dims=((1,), (0,))):
    (ah, al), (bh, bl) = split(a), split(b)
    return mm(ah, bh, dims) + (mm(ah, bl, dims) + mm(al, bh, dims))


def kernel(feat, weight, cot, tiles, cnt, blks, hid_o, gw_o, gf_o,
           G, T, W, C, Ahi, Alo, AThi, ATlo, Pb, Rb, St, Bk, Rs, Es, Ec, Er, Ho, Fo,
           wt, ws, wc, wr, wz, wzr, gw,
           loc_sem, a_s, a_r, b_s, b_r, st_r, d_s, d_r, e_s, e_r, g_s, g_r):
    blk = T.shape[2]
    secs = T.shape[0]
    reps = Pb.shape[1]
    chips = secs // 2
    quarter = reps * blk
    row = lax.axis_index("rows")
    z = lax.axis_index("rep")
    c = row % 2
    q = row // 2
    x = q % 2
    y = q // 2
    sib = row + 1 - 2 * c
    xn = row + 2 - 4 * x
    yn = row + 4 - 8 * y
    dg = xn + yn - row
    plane = (dg, xn, yn)
    zs = [(z + d) % reps for d in range(1, reps)]
    near = z + 1 - 2 * (z % 2)
    far = (z + 2) % reps
    mir = reps - 1 - z
    inner = (z == 1) | (z == 2)
    outer = (z == 0) | (z == 3)

    barrier = pltpu.get_barrier_semaphore()
    peers = [(sib, z)] + [(p, z) for p in plane] + [(row, k) for k in zs]
    for dev in peers:
        pl.semaphore_signal(barrier, inc=1, device_id=dev, device_id_type=MESH)
    loads = [pltpu.make_async_copy(feat.at[:, h * blk:(h + 1) * blk], G.at[h, row], loc_sem.at[h]) for h in range(2)]
    loads += [pltpu.make_async_copy(tiles.at[0, 0], T, loc_sem.at[2]),
              pltpu.make_async_copy(weight, W, loc_sem.at[3]),
              pltpu.make_async_copy(cot, C, loc_sem.at[4])]
    for ld in loads:
        ld.start()
    pl.semaphore_wait(barrier, len(peers))

    sent = []

    def put(src, dst, ss, rs, dev):
        return pltpu.make_async_remote_copy(src_ref=src, dst_ref=dst, send_sem=ss, recv_sem=rs,
                                            device_id=dev, device_id_type=MESH)

    def send(src, dst, ss, rs, dev):
        cp = pltpu.make_async_remote_copy(src_ref=src, dst_ref=dst, send_sem=ss, recv_sem=rs,
                                          device_id=dev, device_id_type=MESH)
        cp.start()
        sent.append(cp)
        return cp

    def drain():
        while sent:
            sent.pop(0).wait_send()

    a_cp = []

    def gather(h):
        loads[h].wait()
        mine = G.at[h, row]
        a_cp.append([send(mine, mine, a_s.at[h, i], a_r.at[h, i], (p, z)) for i, p in enumerate((dg, xn, yn, sib))])

    gather(0)

    loads[2].wait()

    def masks(s, k):
        n = cnt[0, 0, s]
        return [jnp.where((blks[0, 0, t, s] == k) & (t < n), 1.0, 0.0).astype(F32) for t in range(T.shape[1])]

    @pl.loop(0, secs)
    def _(s):
        for k in range(reps):
            m = masks(s, k)
            val = T[s, 0] * m[0]
            for t in range(1, T.shape[1]):
                val = val + T[s, t] * m[t]
            hi, lo = split(val)
            cols = pl.ds(pl.multiple_of(s * blk, blk), blk)
            Ahi[k * blk:(k + 1) * blk, cols] = hi
            Alo[k * blk:(k + 1) * blk, cols] = lo

    drain()
    gather(1)

    rh = blk // 2
    b_pc = ((0, 0, blk), (1, 0, rh), (1, rh, rh))
    d_pc = ((0, 0, rh), (0, rh, rh), (1, 0, blk))

    def b_put(n, k, slot, dev):
        h, at, size = b_pc[n]
        return put(Pb.at[h, k, at:at + size], Rb.at[h, slot, at:at + size], b_s.at[n, slot], b_r.at[n, slot], (row, dev))

    def stage_put(n):
        h, at, size = b_pc[n]
        return put(Pb.at[h, mir, at:at + size], St.at[h, at:at + size], b_s.at[n, 2], st_r.at[n], (row, near))

    def b_send(n):
        @pl.when(outer)
        def _():
            stage_put(n).start()
            b_put(n, far, 1, far).start()
            b_put(n, near, 0, near).start()

        @pl.when(inner)
        def _():
            b_put(n, mir, 2, mir).start()
            b_put(n, near, 0, near).start()

    def combine(n):
        h, at, size = b_pc[n]

        @pl.when(inner)
        def _():
            stage_put(n).wait_recv()
            Pb[h, far, at:at + size] = Pb[h, far, at:at + size] + St[h, at:at + size]
            b_put(n, far, 1, far).start()

    def b_sum(n):
        h, at, size = b_pc[n]
        b_put(n, near, 0, near).wait_recv()
        part = Pb[h, z, at:at + size] + Rb[h, 0, at:at + size]

        @pl.when(inner)
        def _():
            b_put(n, mir, 2, mir).wait_recv()

        @pl.when(outer)
        def _():
            Rb[h, 2, at:at + size] = jnp.zeros((size, blk), F32)

        part = part + Rb[h, 2, at:at + size]
        b_put(n, far, 1, far).wait_recv()
        return part + Rb[h, 1, at:at + size]

    for h in range(2):
        fwd = []
        for i, p in ((1, xn), (2, yn), (0, dg)):
            a_cp[h][i].wait_recv()
            fwd.append(send(G.at[h, p], G.at[h, p], a_s.at[h, 4 + i], a_r.at[h, 4 + i], (sib, z)))
        a_cp[h][3].wait_recv()
        if h == 1:
            combine(0)
        for cp in fwd:
            cp.wait_recv()
        fh, fl = split(G[h].reshape(secs * blk, blk))
        rhs = jnp.concatenate([fh, fl], axis=1)
        acc = mm(Ahi[...], rhs)
        acc = acc[:, :blk] + (acc[:, blk:] + mm(Alo[...], fh))
        Pb[h] = acc.reshape(reps, blk, blk)
        for n in ((0,), (1, 2))[h]:
            b_send(n)

    @pl.loop(0, secs)
    def _(s):
        tt = [T[s, t].T for t in range(T.shape[1])]
        rows = pl.ds(pl.multiple_of(((s % 2) * chips + s // 2) * blk, blk), blk)
        for k in range(reps):
            m = masks(s, k)
            val = tt[0] * m[0]
            for t in range(1, T.shape[1]):
                val = val + tt[t] * m[t]
            hi, lo = split(val)
            AThi[rows, k * blk:(k + 1) * blk] = hi
            ATlo[rows, k * blk:(k + 1) * blk] = lo

    combine(1)
    combine(2)
    loads[3].wait()
    loads[4].wait()

    def d_put(n, k, slot, dev):
        h, at, size = d_pc[n]
        ref = Bk.at[h, k, at:at + size]
        return put(ref, ref, d_s.at[n, slot], d_r.at[n, slot], (row, dev))

    def d_send(n):
        d_put(n, z, 2, mir).start()

        @pl.when(outer)
        def _():
            d_put(n, z, 1, far).start()

        d_put(n, z, 0, near).start()

    w = W[...]
    agg0 = b_sum(0)
    pre0 = mm3(agg0, w[:blk])
    agg1, delta = [], []
    for n in (1, 2):
        at = b_pc[n][1]
        agg1.append(b_sum(n))
        pre = pre0[at:at + rh] + mm3(agg1[-1], w[blk:])
        sig = 1.0 / (1.0 + jnp.exp(-pre))
        delta.append(C[at:at + rh] * (sig * (1.0 + pre * (1.0 - sig))))
        back = mm3(delta[-1], w, ((1,), (1,)))
        for h in range(2):
            Bk[h, z, at:at + rh] = back[:, h * blk:(h + 1) * blk]
        d_send(n - 1)
        Ho[at:at + rh] = pre * sig
    agg = jnp.concatenate([agg0, jnp.concatenate(agg1, axis=0)], axis=1)
    delta = jnp.concatenate(delta, axis=0)
    hid_cp = pltpu.make_async_copy(Ho, hid_o, loc_sem.at[5])
    hid_cp.start()

    def relay(n):
        @pl.when(inner)
        def _():
            d_put(n, mir, 2, mir).wait_recv()
            d_put(n, mir, 1, near).start()


    wt[...] = mm3(agg.T, delta) * (1.0 / math.sqrt(blk * secs * reps))
    half = wt.shape[0] // 2
    piece = half // chips
    sub = piece // reps
    oth = pl.multiple_of((1 - c) * half, half)
    own = pl.multiple_of(c * half, half)
    g1 = send(wt.at[pl.ds(oth, half)], ws, g_s.at[0], g_r.at[0], (sib, z))
    relay(0)
    relay(1)
    for n in (0, 1):
        for i in range(3):
            d_put(n, z, i, near).wait_send()
    d_send(2)
    drain()
    for n in range(3):
        for i in range(3):
            b_put(n, z, i, near).wait_send()
    g1.wait_recv()
    wc[...] = wt[pl.ds(own, half)] + ws[...]
    g2 = [send(wc.at[pl.ds(pl.multiple_of((p // 2) * piece, piece), piece)], wr.at[i], g_s.at[1 + i], g_r.at[1 + i], (p, z))
          for i, p in enumerate(plane)]

    def rows_start(h):
        for n in ((0, 1), (2,))[h]:
            d_put(n, near, 0, near).wait_recv()
            d_put(n, far, 1, far).wait_recv()

        @pl.when(outer)
        def _():
            for n in ((0, 1), (2,))[h]:
                d_put(n, mir, 2, mir).wait_recv()

        bh, bl = split(Bk[h].reshape(quarter, blk))
        rhs = jnp.concatenate([bh, bl], axis=1)
        out = None
        for first, core in ((True, 1 - c), (False, c)):
            at = pl.ds(pl.multiple_of(core * (chips * blk), chips * blk), chips * blk)
            acc = mm(AThi[at], rhs)
            acc = acc[:, :blk] + (acc[:, blk:] + mm(ATlo[at], bh))
            Rs[h, 0 if first else 1] = acc.reshape(chips, blk, blk)
            if first:
                out = [send(Rs.at[h, 0, p // 2], Es.at[h, p // 2], e_s.at[h, 3 + i], e_r.at[h, 3 + i], (sib, z))
                       for i, p in enumerate((dg, xn, yn, row))]
        return out

    def rows_mid(h, cps):
        out = []
        for i, p in enumerate((dg, xn, yn)):
            cps[i].wait_recv()
            Ec[h, i] = Rs[h, 1, p // 2] + Es[h, p // 2]
            out.append(send(Ec.at[h, i], Er.at[h, i], e_s.at[h, i], e_r.at[h, i], (p, z)))
        cps[3].wait_recv()
        return out

    def rows_end(h, cps):
        total = Rs[h, 1, q] + Es[h, q]
        for i, cp in enumerate(cps):
            cp.wait_recv()
            total = total + Er[h, i]
        Fo[:, h * blk:(h + 1) * blk] = total

    e0 = rows_start(0)
    relay(2)
    e0 = rows_mid(0, e0)

    at = pl.multiple_of(q * piece, piece)
    total = wc[pl.ds(at, piece)]
    for i in range(3):
        g2[i].wait_recv()
        total = total + wr[i]
    wz[...] = total
    g3 = [send(wz.at[pl.ds(pl.multiple_of(k * sub, sub), sub)], wzr.at[i], g_s.at[4 + i], g_r.at[4 + i], (row, k))
          for i, k in enumerate(zs)]

    total = wz[pl.ds(pl.multiple_of(z * sub, sub), sub)]
    for i in range(reps - 1):
        g3[i].wait_recv()
        total = total + wzr[i]
    top = c * half + q * piece
    mine = pl.ds(pl.multiple_of(top + z * sub, sub), sub)
    gw[mine] = total
    g4 = [send(gw.at[mine], gw.at[mine], g_s.at[7 + i], g_r.at[7 + i], (row, k)) for i, k in enumerate(zs)]
    e1 = rows_start(1)
    for cp in g4:
        cp.wait_recv()
    mine = pl.ds(pl.multiple_of(top, piece), piece)
    g5 = [send(gw.at[mine], gw.at[mine], g_s.at[10 + i], g_r.at[10 + i], (p, z)) for i, p in enumerate(plane)]

    e1 = rows_mid(1, e1)
    rows_end(0, e0)

    for cp in g5:
        cp.wait_recv()
    mine = pl.ds(own, half)
    g6 = send(gw.at[mine], gw.at[mine], g_s.at[13], g_r.at[13], (sib, z))

    rows_end(1, e1)
    f_cp = pltpu.make_async_copy(Fo, gf_o, loc_sem.at[6])
    f_cp.start()
    g6.wait_recv()
    g_cp = pltpu.make_async_copy(gw, gw_o, loc_sem.at[7])
    g_cp.start()
    drain()
    for i in range(3):
        d_put(2, z, i, near).wait_send()
    hid_cp.wait()
    f_cp.wait()
    g_cp.wait()


def store(a, b, c, x, y, z, u, v, w, sem):
    bufs = ((a, u, x), (b, v, y), (c, w, z))
    ins = [pltpu.make_async_copy(s, t, sem.at[0, i]) for i, (s, t, _) in enumerate(bufs)]
    outs = [pltpu.make_async_copy(t, d, sem.at[1, i]) for i, (_, t, d) in enumerate(bufs)]
    for cp in ins:
        cp.start()
    for cp, out in zip(ins, outs):
        cp.wait()
        out.start()
    for out in outs:
        out.wait()


def fused(features, weight, cotangent, tiles, tile_count, tile_block):
    blk, width = features.shape
    secs, slots = tiles.shape[2], tiles.shape[3]
    reps = lax.axis_size("rep")
    chips = secs // 2
    half = width // 2
    piece = half // chips
    sub = piece // reps
    V = pltpu.VMEM
    dma = pltpu.SemaphoreType.DMA
    hbm = pl.BlockSpec(memory_space=pltpu.HBM)
    smem = pl.BlockSpec(memory_space=pltpu.SMEM)
    flops = 2 * 3 * 2 * (reps * blk) * (secs * blk) * width
    raw = pl.pallas_call(
        kernel,
        out_shape=(jax.ShapeDtypeStruct((blk, width), F32), jax.ShapeDtypeStruct((width, width), F32),
                   jax.ShapeDtypeStruct((blk, width), F32)),
        in_specs=[hbm, hbm, hbm, hbm, smem, smem],
        out_specs=(hbm,) * 3,
        scratch_shapes=[
            V((2, secs, blk, blk), F32), V((secs, slots, blk, blk), F32), V((width, width), F32), V((blk, width), F32),
            V((reps * blk, secs * blk), BF16), V((reps * blk, secs * blk), BF16),
            V((secs * blk, reps * blk), BF16), V((secs * blk, reps * blk), BF16),
            V((2, reps, blk, blk), F32), V((2, reps - 1, blk, blk), F32), V((2, blk, blk), F32), V((2, reps, blk, blk), F32),
            V((2, 2, chips, blk, blk), F32), V((2, chips, blk, blk), F32), V((2, 3, blk, blk), F32), V((2, 3, blk, blk), F32),
            V((blk, width), F32), V((blk, width), F32),
            V((width, width), F32), V((half, width), F32), V((half, width), F32), V((3, piece, width), F32),
            V((piece, width), F32), V((reps - 1, sub, width), F32), V((width, width), F32),
            dma((8,)), dma((2, 7)), dma((2, 7)), dma((3, 3)), dma((3, 3)), dma((3,)), dma((3, 3)), dma((3, 3)),
            dma((2, 7)), dma((2, 7)), dma((14,)), dma((14,)),
        ],
        compiler_params=pltpu.CompilerParams(collective_id=0, has_side_effects=True, vmem_limit_bytes=LIMIT),
        cost_estimate=pl.CostEstimate(flops=flops, bytes_accessed=4 * tiles.size, transcendentals=blk * width),
        name="graph_step",
    )(features, weight, cotangent, tiles, tile_count, tile_block.transpose(0, 1, 3, 2))
    return pl.pallas_call(
        store,
        out_shape=tuple(jax.ShapeDtypeStruct(r.shape, r.dtype) for r in raw),
        in_specs=[hbm] * 3,
        out_specs=(hbm,) * 3,
        scratch_shapes=[V(r.shape, r.dtype) for r in raw] + [dma((2, 3))],
        compiler_params=pltpu.CompilerParams(vmem_limit_bytes=LIMIT),
        name="store_results",
    )(*raw)


def silu_slope(pre):
    sig = jax.nn.sigmoid(pre)
    return sig * (1.0 + pre * (1.0 - sig))


def body(features, weight, cotangent, tiles, tile_count, tile_block):
    highest = lax.Precision.HIGHEST
    tile_set = tiles[0, 0]
    counts = tile_count[0, 0]
    block_ids = tile_block[0, 0]
    sections = tile_set.shape[0]
    slots = tile_set.shape[1]
    blk = tile_set.shape[2]
    width = features.shape[1]
    groups = lax.axis_size("rep")
    select = (
        (block_ids[..., None] == jnp.arange(groups, dtype=jnp.int32))
        & (jnp.arange(slots, dtype=jnp.int32)[:, None] < counts[:, None, None])
    ).astype(jnp.float32)
    gathered = lax.all_gather(features, "rows", axis=0, tiled=True).reshape(sections, blk, width)
    prods = jnp.einsum("stab,sbf->staf", tile_set, gathered, precision=highest)
    total = jnp.einsum("stk,staf->kaf", select, prods, precision=highest)
    aggregated = lax.psum_scatter(
        total.reshape(groups * blk, width), "rep", scatter_dimension=0, tiled=True
    )
    pre = jnp.dot(aggregated, weight, precision=highest)
    hidden = jax.nn.silu(pre)
    delta = cotangent * silu_slope(pre)
    weight_term = jnp.dot(aggregated.T, delta, precision=highest)
    node_total = blk * lax.axis_size("rows") * groups
    grad_weight = lax.psum(weight_term, ("rows", "rep")) / math.sqrt(node_total)
    back = jnp.dot(delta, weight.T, precision=highest)
    group_back = lax.all_gather(back, "rep", axis=0, tiled=True).reshape(groups, blk, width)
    count = sections * blk
    picked = jnp.einsum("stk,kaf->staf", select, group_back, precision=highest)
    result = jnp.einsum("stab,staf->sbf", tile_set, picked, precision=highest)
    all_terms = result.reshape(count, width)
    grad_features = lax.psum_scatter(all_terms, "rows", scatter_dimension=0, tiled=True)
    return (hidden, grad_weight, grad_features)


def solution(mesh):
    in_specs = (
        P(("rows", "rep"), None),
        P(),
        P(("rows", "rep"), None),
        P("rows", "rep", None, None, None, None),
        P("rows", "rep", None),
        P("rows", "rep", None, None),
    )
    out_specs = (P(("rows", "rep"), None), P(), P(("rows", "rep"), None))
    fits = mesh.shape["rows"] == 8 and mesh.shape["rep"] == 4
    return jax.shard_map(fused if fits else body, mesh=mesh, in_specs=in_specs, out_specs=out_specs, check_vma=False)
```

```python
import functools
import math

import jax
import jax.numpy as jnp
from jax import lax
from jax.experimental import pallas as pl
from jax.experimental.pallas import tpu as pltpu
from jax.sharding import PartitionSpec as P

LIMIT = 60 * 1024 * 1024
MESH = pl.DeviceIdType.MESH
F32 = jnp.float32
BF16 = jnp.bfloat16


def split(x):
    hi = x.astype(BF16)
    return hi, (x - hi.astype(F32)).astype(BF16)


def mm(a, b, dims=((1,), (0,))):
    return lax.dot_general(a, b, (dims, ((), ())), preferred_element_type=F32)


def mm3(a, b, dims=((1,), (0,))):
    (ah, al), (bh, bl) = split(a), split(b)
    return mm(ah, bh, dims) + (mm(ah, bl, dims) + mm(al, bh, dims))


def kernel(feat, weight, cot, tiles, cnt, blks, hid_o, gw_o, gf_o,
           G, T, W, C, Ahi, Alo, AThi, ATlo, Pb, Rb, St, Bk, Rs, Es, Ec, Er, Ho, Fo,
           wt, ws, wc, wr, wz, wzr, gw,
           loc_sem, a_s, a_r, b_s, b_r, st_r, d_s, d_r, e_s, e_r, g_s, g_r):
    blk = T.shape[2]
    secs = T.shape[0]
    reps = Pb.shape[1]
    chips = secs // 2
    quarter = reps * blk
    row = lax.axis_index("rows")
    z = lax.axis_index("rep")
    c = row % 2
    q = row // 2
    x = q % 2
    y = q // 2
    sib = row + 1 - 2 * c
    xn = row + 2 - 4 * x
    yn = row + 4 - 8 * y
    dg = xn + yn - row
    plane = (dg, xn, yn)
    zs = [(z + d) % reps for d in range(1, reps)]
    near = z + 1 - 2 * (z % 2)
    far = (z + 2) % reps
    mir = reps - 1 - z
    inner = (z == 1) | (z == 2)
    outer = (z == 0) | (z == 3)

    barrier = pltpu.get_barrier_semaphore()
    peers = [(sib, z)] + [(p, z) for p in plane] + [(row, k) for k in zs]
    for dev in peers:
        pl.semaphore_signal(barrier, inc=1, device_id=dev, device_id_type=MESH)
    loads = [pltpu.make_async_copy(feat.at[:, h * blk:(h + 1) * blk], G.at[h, row], loc_sem.at[h]) for h in range(2)]
    loads += [pltpu.make_async_copy(tiles.at[0, 0], T, loc_sem.at[2]),
              pltpu.make_async_copy(weight, W, loc_sem.at[3]),
              pltpu.make_async_copy(cot, C, loc_sem.at[4])]
    for ld in loads:
        ld.start()
    pl.semaphore_wait(barrier, len(peers))

    sent = []

    def put(src, dst, ss, rs, dev):
        return pltpu.make_async_remote_copy(src_ref=src, dst_ref=dst, send_sem=ss, recv_sem=rs,
                                            device_id=dev, device_id_type=MESH)

    def send(src, dst, ss, rs, dev):
        cp = pltpu.make_async_remote_copy(src_ref=src, dst_ref=dst, send_sem=ss, recv_sem=rs,
                                          device_id=dev, device_id_type=MESH)
        cp.start()
        sent.append(cp)
        return cp

    def drain():
        while sent:
            sent.pop(0).wait_send()

    a_cp = []

    def gather(h):
        loads[h].wait()
        mine = G.at[h, row]
        a_cp.append([send(mine, mine, a_s.at[h, i], a_r.at[h, i], (p, z)) for i, p in ((3, dg), (1, xn), (2, yn), (0, sib))])

    gather(0)
    gather(1)

    loads[2].wait()

    def masks(s, k):
        n = cnt[0, 0, s]
        return [jnp.where((blks[0, 0, t, s] == k) & (t < n), 1.0, 0.0).astype(F32) for t in range(T.shape[1])]

    @pl.loop(0, secs)
    def _(s):
        for k in range(reps):
            m = masks(s, k)
            val = T[s, 0] * m[0]
            for t in range(1, T.shape[1]):
                val = val + T[s, t] * m[t]
            hi, lo = split(val)
            cols = pl.ds(pl.multiple_of(s * blk, blk), blk)
            Ahi[k * blk:(k + 1) * blk, cols] = hi
            Alo[k * blk:(k + 1) * blk, cols] = lo

    rh = blk // 2
    b_pc = ((0, 0, blk), (1, 0, rh), (1, rh, rh))
    d_pc = ((0, 0, rh), (0, rh, rh), (1, 0, blk))

    def b_put(n, k, slot, dev):
        h, at, size = b_pc[n]
        return put(Pb.at[h, k, at:at + size], Rb.at[h, slot, at:at + size], b_s.at[n, slot], b_r.at[n, slot], (row, dev))

    def stage_put(n):
        h, at, size = b_pc[n]
        return put(Pb.at[h, mir, at:at + size], St.at[h, at:at + size], b_s.at[n, 2], st_r.at[n], (row, near))

    def b_send(n):
        @pl.when(outer)
        def _():
            stage_put(n).start()
            b_put(n, far, 1, far).start()
            b_put(n, near, 0, near).start()

        @pl.when(inner)
        def _():
            b_put(n, mir, 2, mir).start()
            b_put(n, near, 0, near).start()

    def combine(n):
        h, at, size = b_pc[n]

        @pl.when(inner)
        def _():
            stage_put(n).wait_recv()
            Pb[h, far, at:at + size] = Pb[h, far, at:at + size] + St[h, at:at + size]
            b_put(n, far, 1, far).start()

    def b_sum(n):
        h, at, size = b_pc[n]
        b_put(n, near, 0, near).wait_recv()
        part = Pb[h, z, at:at + size] + Rb[h, 0, at:at + size]

        @pl.when(inner)
        def _():
            b_put(n, mir, 2, mir).wait_recv()

        @pl.when(outer)
        def _():
            Rb[h, 2, at:at + size] = jnp.zeros((size, blk), F32)

        part = part + Rb[h, 2, at:at + size]
        b_put(n, far, 1, far).wait_recv()
        return part + Rb[h, 1, at:at + size]

    def pair_rhs(ref):
        hi, lo = split(ref.reshape(2 * blk, blk))
        return jnp.concatenate([hi, lo], axis=1)

    def pair_mm(ah, al, rhs):
        acc = mm(ah, rhs)
        return acc[:, :blk] + (acc[:, blk:] + mm(al, rhs[:, :blk]))

    def add_chip(h, chip, first=False):
        cols = pl.ds(pl.multiple_of(chip * (2 * blk), 2 * blk), 2 * blk)
        part = pair_mm(Ahi[:, cols], Alo[:, cols], pair_rhs(G[h, pl.ds(2 * chip, 2)])).reshape(reps, blk, blk)
        Pb[h] = part if first else Pb[h] + part

    for h in range(2):

        def forward(i, p):
            put(G.at[h, p], G.at[h, p], a_s.at[h, i], a_r.at[h, i], (p, z)).wait_recv()
            send(G.at[h, p], G.at[h, p], a_s.at[h, 3 + i], a_r.at[h, 3 + i], (sib, z))

        forward(1, xn)
        forward(2, yn)
        a_cp[h][3].wait_recv()
        add_chip(h, q, True)
        forward(3, dg)
        if h == 1:
            combine(0)

        @pl.loop(1, 4)
        def _(i):
            p = row + (i % 2) * (2 - 4 * x) + (i // 2) * (4 - 8 * y)
            put(G.at[h, p], G.at[h, p], a_s.at[h, 3 + i], a_r.at[h, 3 + i], (sib, z)).wait_recv()
            add_chip(h, p // 2)

        for n in ((0,), (1, 2))[h]:
            b_send(n)

    @pl.loop(0, secs)
    def _(s):
        tt = [T[s, t].T for t in range(T.shape[1])]
        rows = pl.ds(pl.multiple_of(((s % 2) * chips + s // 2) * blk, blk), blk)
        for k in range(reps):
            m = masks(s, k)
            val = tt[0] * m[0]
            for t in range(1, T.shape[1]):
                val = val + tt[t] * m[t]
            hi, lo = split(val)
            AThi[rows, k * blk:(k + 1) * blk] = hi
            ATlo[rows, k * blk:(k + 1) * blk] = lo

    combine(1)
    combine(2)
    loads[3].wait()
    loads[4].wait()

    def d_put(n, k, slot, dev):
        h, at, size = d_pc[n]
        ref = Bk.at[h, k, at:at + size]
        return put(ref, ref, d_s.at[n, slot], d_r.at[n, slot], (row, dev))

    def d_send(n):
        d_put(n, z, 2, mir).start()

        @pl.when(outer)
        def _():
            d_put(n, z, 1, far).start()

        d_put(n, z, 0, near).start()

    w = W[...]
    agg0 = b_sum(0)
    pre0 = mm3(agg0, w[:blk])
    agg1, delta = [], []
    for n in (1, 2):
        at = b_pc[n][1]
        agg1.append(b_sum(n))
        pre = pre0[at:at + rh] + mm3(agg1[-1], w[blk:])
        sig = 1.0 / (1.0 + jnp.exp(-pre))
        delta.append(C[at:at + rh] * (sig * (1.0 + pre * (1.0 - sig))))
        back = mm3(delta[-1], w, ((1,), (1,)))
        for h in range(2):
            Bk[h, z, at:at + rh] = back[:, h * blk:(h + 1) * blk]
        d_send(n - 1)
        Ho[at:at + rh] = pre * sig
    d_send(2)
    agg = jnp.concatenate([agg0, jnp.concatenate(agg1, axis=0)], axis=1)
    delta = jnp.concatenate(delta, axis=0)
    hid_cp = pltpu.make_async_copy(Ho, hid_o, loc_sem.at[5])
    hid_cp.start()

    def relay(n):
        @pl.when(inner)
        def _():
            d_put(n, mir, 2, mir).wait_recv()
            d_put(n, mir, 1, near).start()


    wt[...] = mm3(agg.T, delta) * (1.0 / math.sqrt(blk * secs * reps))
    half = wt.shape[0] // 2
    piece = half // chips
    sub = piece // reps
    oth = pl.multiple_of((1 - c) * half, half)
    own = pl.multiple_of(c * half, half)
    g1 = send(wt.at[pl.ds(oth, half)], ws, g_s.at[0], g_r.at[0], (sib, z))
    relay(0)
    relay(1)
    drain()
    for n in range(3):
        for i in range(3):
            b_put(n, z, i, near).wait_send()
    g1.wait_recv()
    wc[...] = wt[pl.ds(own, half)] + ws[...]
    g2 = [send(wc.at[pl.ds(pl.multiple_of((p // 2) * piece, piece), piece)], wr.at[i], g_s.at[1 + i], g_r.at[1 + i], (p, z))
          for i, p in enumerate(plane)]

    def rows_start(h):
        parts = ((0, 1 - c), (1, c))
        at = [pl.ds(pl.multiple_of(core * (chips * blk), chips * blk), chips * blk) for _, core in parts]

        def pair(k):
            cols = pl.ds(pl.multiple_of(k * blk, 2 * blk), 2 * blk)
            rhs = pair_rhs(Bk[h, pl.ds(k, 2)])
            return [lambda a=a: pair_mm(AThi[a, cols], ATlo[a, cols], rhs).reshape(chips, blk, blk) for a in at]

        pieces = ((0, 1), (2,))[h]
        for n in pieces:
            d_put(n, near, 0, near).wait_recv()
        here = (z // 2) * 2
        for i, part in enumerate(pair(here)):
            Rs[h, i] = part()
        for n in pieces:
            d_put(n, far, 1, far).wait_recv()

        @pl.when(outer)
        def _():
            for n in pieces:
                d_put(n, mir, 2, mir).wait_recv()

        out = []
        for i, part in enumerate(pair(2 - here)):
            Rs[h, i] = Rs[h, i] + part()
            if i == 0:
                out = [send(Rs.at[h, 0, p // 2], Es.at[h, p // 2], e_s.at[h, 3 + m], e_r.at[h, 3 + m], (sib, z))
                       for m, p in enumerate((dg, xn, yn, row))]
        return out

    def rows_mid(h, cps):
        out = []
        for i, p in enumerate((dg, xn, yn)):
            cps[i].wait_recv()
            Ec[h, i] = Rs[h, 1, p // 2] + Es[h, p // 2]
            out.append(send(Ec.at[h, i], Er.at[h, i], e_s.at[h, i], e_r.at[h, i], (p, z)))
        cps[3].wait_recv()
        return out

    def rows_end(h, cps):
        total = Rs[h, 1, q] + Es[h, q]
        for i, cp in enumerate(cps):
            cp.wait_recv()
            total = total + Er[h, i]
        Fo[:, h * blk:(h + 1) * blk] = total

    e0 = rows_start(0)
    relay(2)
    e0 = rows_mid(0, e0)

    at = pl.multiple_of(q * piece, piece)
    total = wc[pl.ds(at, piece)]
    for i in range(3):
        g2[i].wait_recv()
        total = total + wr[i]
    wz[...] = total
    g3 = [send(wz.at[pl.ds(pl.multiple_of(k * sub, sub), sub)], wzr.at[i], g_s.at[4 + i], g_r.at[4 + i], (row, k))
          for i, k in enumerate(zs)]

    total = wz[pl.ds(pl.multiple_of(z * sub, sub), sub)]
    for i in range(reps - 1):
        g3[i].wait_recv()
        total = total + wzr[i]
    top = c * half + q * piece
    mine = pl.ds(pl.multiple_of(top + z * sub, sub), sub)
    gw[mine] = total
    g4 = [send(gw.at[mine], gw.at[mine], g_s.at[7 + i], g_r.at[7 + i], (row, k)) for i, k in enumerate(zs)]
    e1 = rows_start(1)
    for cp in g4:
        cp.wait_recv()
    mine = pl.ds(pl.multiple_of(top, piece), piece)
    g5 = [send(gw.at[mine], gw.at[mine], g_s.at[10 + i], g_r.at[10 + i], (p, z)) for i, p in enumerate(plane)]

    e1 = rows_mid(1, e1)
    rows_end(0, e0)

    for cp in g5:
        cp.wait_recv()
    mine = pl.ds(own, half)
    g6 = send(gw.at[mine], gw.at[mine], g_s.at[13], g_r.at[13], (sib, z))

    rows_end(1, e1)
    f_cp = pltpu.make_async_copy(Fo, gf_o, loc_sem.at[6])
    f_cp.start()
    g6.wait_recv()
    g_cp = pltpu.make_async_copy(gw, gw_o, loc_sem.at[7])
    g_cp.start()
    drain()
    for n in range(3):
        for i in range(3):
            d_put(n, z, i, near).wait_send()
    hid_cp.wait()
    f_cp.wait()
    g_cp.wait()


def store(a, b, c, x, y, z, u, v, w, sem):
    bufs = ((a, u, x), (b, v, y), (c, w, z))
    ins = [pltpu.make_async_copy(s, t, sem.at[0, i]) for i, (s, t, _) in enumerate(bufs)]
    outs = [pltpu.make_async_copy(t, d, sem.at[1, i]) for i, (_, t, d) in enumerate(bufs)]
    for cp in ins:
        cp.start()
    for cp, out in zip(ins, outs):
        cp.wait()
        out.start()
    for out in outs:
        out.wait()


def fused(features, weight, cotangent, tiles, tile_count, tile_block):
    blk, width = features.shape
    secs, slots = tiles.shape[2], tiles.shape[3]
    reps = lax.axis_size("rep")
    chips = secs // 2
    half = width // 2
    piece = half // chips
    sub = piece // reps
    V = pltpu.VMEM
    dma = pltpu.SemaphoreType.DMA
    hbm = pl.BlockSpec(memory_space=pltpu.HBM)
    smem = pl.BlockSpec(memory_space=pltpu.SMEM)
    flops = 2 * 3 * 2 * (reps * blk) * (secs * blk) * width
    raw = pl.pallas_call(
        kernel,
        out_shape=(jax.ShapeDtypeStruct((blk, width), F32), jax.ShapeDtypeStruct((width, width), F32),
                   jax.ShapeDtypeStruct((blk, width), F32)),
        in_specs=[hbm, hbm, hbm, hbm, smem, smem],
        out_specs=(hbm,) * 3,
        scratch_shapes=[
            V((2, secs, blk, blk), F32), V((secs, slots, blk, blk), F32), V((width, width), F32), V((blk, width), F32),
            V((reps * blk, secs * blk), BF16), V((reps * blk, secs * blk), BF16),
            V((secs * blk, reps * blk), BF16), V((secs * blk, reps * blk), BF16),
            V((2, reps, blk, blk), F32), V((2, reps - 1, blk, blk), F32), V((2, blk, blk), F32), V((2, reps, blk, blk), F32),
            V((2, 2, chips, blk, blk), F32), V((2, chips, blk, blk), F32), V((2, 3, blk, blk), F32), V((2, 3, blk, blk), F32),
            V((blk, width), F32), V((blk, width), F32),
            V((width, width), F32), V((half, width), F32), V((half, width), F32), V((3, piece, width), F32),
            V((piece, width), F32), V((reps - 1, sub, width), F32), V((width, width), F32),
            dma((8,)), dma((2, 7)), dma((2, 7)), dma((3, 3)), dma((3, 3)), dma((3,)), dma((3, 3)), dma((3, 3)),
            dma((2, 7)), dma((2, 7)), dma((14,)), dma((14,)),
        ],
        compiler_params=pltpu.CompilerParams(collective_id=0, has_side_effects=True, vmem_limit_bytes=LIMIT),
        cost_estimate=pl.CostEstimate(flops=flops, bytes_accessed=4 * tiles.size, transcendentals=blk * width),
        name="graph_step",
    )(features, weight, cotangent, tiles, tile_count, tile_block.transpose(0, 1, 3, 2))
    return pl.pallas_call(
        store,
        out_shape=tuple(jax.ShapeDtypeStruct(r.shape, r.dtype) for r in raw),
        in_specs=[hbm] * 3,
        out_specs=(hbm,) * 3,
        scratch_shapes=[V(r.shape, r.dtype) for r in raw] + [dma((2, 3))],
        compiler_params=pltpu.CompilerParams(vmem_limit_bytes=LIMIT),
        name="store_results",
    )(*raw)


def silu_slope(pre):
    sig = jax.nn.sigmoid(pre)
    return sig * (1.0 + pre * (1.0 - sig))


def body(features, weight, cotangent, tiles, tile_count, tile_block):
    highest = lax.Precision.HIGHEST
    tile_set = tiles[0, 0]
    counts = tile_count[0, 0]
    block_ids = tile_block[0, 0]
    sections = tile_set.shape[0]
    slots = tile_set.shape[1]
    blk = tile_set.shape[2]
    width = features.shape[1]
    groups = lax.axis_size("rep")
    select = (
        (block_ids[..., None] == jnp.arange(groups, dtype=jnp.int32))
        & (jnp.arange(slots, dtype=jnp.int32)[:, None] < counts[:, None, None])
    ).astype(jnp.float32)
    gathered = lax.all_gather(features, "rows", axis=0, tiled=True).reshape(sections, blk, width)
    prods = jnp.einsum("stab,sbf->staf", tile_set, gathered, precision=highest)
    total = jnp.einsum("stk,staf->kaf", select, prods, precision=highest)
    aggregated = lax.psum_scatter(
        total.reshape(groups * blk, width), "rep", scatter_dimension=0, tiled=True
    )
    pre = jnp.dot(aggregated, weight, precision=highest)
    hidden = jax.nn.silu(pre)
    delta = cotangent * silu_slope(pre)
    weight_term = jnp.dot(aggregated.T, delta, precision=highest)
    node_total = blk * lax.axis_size("rows") * groups
    grad_weight = lax.psum(weight_term, ("rows", "rep")) / math.sqrt(node_total)
    back = jnp.dot(delta, weight.T, precision=highest)
    group_back = lax.all_gather(back, "rep", axis=0, tiled=True).reshape(groups, blk, width)
    count = sections * blk
    picked = jnp.einsum("stk,kaf->staf", select, group_back, precision=highest)
    result = jnp.einsum("stab,staf->sbf", tile_set, picked, precision=highest)
    all_terms = result.reshape(count, width)
    grad_features = lax.psum_scatter(all_terms, "rows", scatter_dimension=0, tiled=True)
    return (hidden, grad_weight, grad_features)


def solution(mesh):
    in_specs = (
        P(("rows", "rep"), None),
        P(),
        P(("rows", "rep"), None),
        P("rows", "rep", None, None, None, None),
        P("rows", "rep", None),
        P("rows", "rep", None, None),
    )
    out_specs = (P(("rows", "rep"), None), P(), P(("rows", "rep"), None))
    fits = mesh.shape["rows"] == 8 and mesh.shape["rep"] == 4
    return jax.shard_map(fused if fits else body, mesh=mesh, in_specs=in_specs, out_specs=out_specs, check_vma=False)
```

```python
import functools
import math

import jax
import jax.numpy as jnp
from jax import lax
from jax.experimental import pallas as pl
from jax.experimental.pallas import tpu as pltpu
from jax.sharding import PartitionSpec as P

LIMIT = 60 * 1024 * 1024
MESH = pl.DeviceIdType.MESH
F32 = jnp.float32
BF16 = jnp.bfloat16


def split(x):
    hi = x.astype(BF16)
    return hi, (x - hi.astype(F32)).astype(BF16)


def mm(a, b, dims=((1,), (0,))):
    return lax.dot_general(a, b, (dims, ((), ())), preferred_element_type=F32)


def mm3(a, b, dims=((1,), (0,))):
    (ah, al), (bh, bl) = split(a), split(b)
    return mm(ah, bh, dims) + (mm(ah, bl, dims) + mm(al, bh, dims))


def kernel(feat, weight, cot, tiles, cnt, blks, hid_o, gw_o, gf_o,
           G, T, W, C, Ahi, Alo, AThi, ATlo, Pb, Rb, St, Bk, Rs, Es, Ec, Er, Ho, Fo,
           wt, ws, wc, wr, wz, wzr, gw,
           loc_sem, a_s, a_r, b_s, b_r, st_r, d_s, d_r, e_s, e_r, g_s, g_r):
    blk = T.shape[2]
    secs = T.shape[0]
    reps = Pb.shape[1]
    chips = secs // 2
    quarter = reps * blk
    row = lax.axis_index("rows")
    z = lax.axis_index("rep")
    c = row % 2
    q = row // 2
    x = q % 2
    y = q // 2
    sib = row + 1 - 2 * c
    xn = row + 2 - 4 * x
    yn = row + 4 - 8 * y
    dg = xn + yn - row
    plane = (dg, xn, yn)
    zs = [(z + d) % reps for d in range(1, reps)]
    near = z + 1 - 2 * (z % 2)
    far = (z + 2) % reps
    mir = reps - 1 - z
    inner = (z == 1) | (z == 2)
    outer = (z == 0) | (z == 3)

    barrier = pltpu.get_barrier_semaphore()
    peers = [(sib, z)] + [(p, z) for p in plane] + [(row, k) for k in zs]
    for dev in peers:
        pl.semaphore_signal(barrier, inc=1, device_id=dev, device_id_type=MESH)
    loads = [pltpu.make_async_copy(feat.at[:, h * blk:(h + 1) * blk], G.at[h, row], loc_sem.at[h]) for h in range(2)]
    loads += [pltpu.make_async_copy(tiles.at[0, 0], T, loc_sem.at[2]),
              pltpu.make_async_copy(weight, W, loc_sem.at[3]),
              pltpu.make_async_copy(cot, C, loc_sem.at[4])]
    for ld in loads:
        ld.start()
    pl.semaphore_wait(barrier, len(peers))

    sent = []

    def put(src, dst, ss, rs, dev):
        return pltpu.make_async_remote_copy(src_ref=src, dst_ref=dst, send_sem=ss, recv_sem=rs,
                                            device_id=dev, device_id_type=MESH)

    def send(src, dst, ss, rs, dev):
        cp = pltpu.make_async_remote_copy(src_ref=src, dst_ref=dst, send_sem=ss, recv_sem=rs,
                                          device_id=dev, device_id_type=MESH)
        cp.start()
        sent.append(cp)
        return cp

    def drain():
        while sent:
            sent.pop(0).wait_send()

    a_cp = []

    def gather(h):
        loads[h].wait()
        mine = G.at[h, row]
        a_cp.append([send(mine, mine, a_s.at[h, i], a_r.at[h, i], (p, z)) for i, p in ((3, dg), (1, xn), (2, yn), (0, sib))])

    gather(0)

    loads[2].wait()

    def masks(s, k):
        n = cnt[0, 0, s]
        return [jnp.where((blks[0, 0, t, s] == k) & (t < n), 1.0, 0.0).astype(F32) for t in range(T.shape[1])]

    @pl.loop(0, secs)
    def _(s):
        for k in range(reps):
            m = masks(s, k)
            val = T[s, 0] * m[0]
            for t in range(1, T.shape[1]):
                val = val + T[s, t] * m[t]
            hi, lo = split(val)
            cols = pl.ds(pl.multiple_of(s * blk, blk), blk)
            Ahi[k * blk:(k + 1) * blk, cols] = hi
            Alo[k * blk:(k + 1) * blk, cols] = lo

    rh = blk // 2
    b_pc = ((0, 0, blk), (1, 0, rh), (1, rh, rh))
    d_pc = ((0, 0, rh), (0, rh, rh), (1, 0, blk))

    def b_put(n, k, slot, dev):
        h, at, size = b_pc[n]
        return put(Pb.at[h, k, at:at + size], Rb.at[h, slot, at:at + size], b_s.at[n, slot], b_r.at[n, slot], (row, dev))

    def stage_put(n):
        h, at, size = b_pc[n]
        return put(Pb.at[h, mir, at:at + size], St.at[h, at:at + size], b_s.at[n, 2], st_r.at[n], (row, near))

    def b_send(n):
        @pl.when(outer)
        def _():
            stage_put(n).start()

        @pl.when(inner)
        def _():
            b_put(n, mir, 2, mir).start()
            b_put(n, near, 0, near).start()

    def combine(n):
        h, at, size = b_pc[n]

        @pl.when(inner)
        def _():
            stage_put(n).wait_recv()
            Pb[h, far, at:at + size] = Pb[h, far, at:at + size] + St[h, at:at + size]
            b_put(n, far, 1, far).start()

        @pl.when(outer)
        def _():
            b_put(n, near, 0, near).wait_recv()
            b_put(n, far, 1, far).start()
            b_put(n, near, 0, near).start()

    def b_sum(n):
        h, at, size = b_pc[n]

        @pl.when(inner)
        def _():
            b_put(n, near, 0, near).wait_recv()
            b_put(n, mir, 2, mir).wait_recv()

        @pl.when(outer)
        def _():
            Rb[h, 2, at:at + size] = jnp.zeros((size, blk), F32)

        part = Pb[h, z, at:at + size] + Rb[h, 0, at:at + size] + Rb[h, 2, at:at + size]
        b_put(n, far, 1, far).wait_recv()
        return part + Rb[h, 1, at:at + size]

    def pair_rhs(ref):
        hi, lo = split(ref.reshape(2 * blk, blk))
        return jnp.concatenate([hi, lo], axis=1)

    def pair_mm(ah, al, rhs):
        acc = mm(ah, rhs)
        return acc[:, :blk] + (acc[:, blk:] + mm(al, rhs[:, :blk]))

    def add_chip(h, chip, first=False):
        cols = pl.ds(pl.multiple_of(chip * (2 * blk), 2 * blk), 2 * blk)
        part = pair_mm(Ahi[:, cols], Alo[:, cols], pair_rhs(G[h, pl.ds(2 * chip, 2)])).reshape(reps, blk, blk)
        Pb[h] = part if first else Pb[h] + part

    for h in range(2):

        def forward(i, p):
            put(G.at[h, p], G.at[h, p], a_s.at[h, i], a_r.at[h, i], (p, z)).wait_recv()
            send(G.at[h, p], G.at[h, p], a_s.at[h, 3 + i], a_r.at[h, 3 + i], (sib, z))

        forward(1, xn)
        forward(2, yn)
        a_cp[h][3].wait_recv()
        add_chip(h, q, True)
        forward(3, dg)
        if h == 0:
            gather(1)
        else:
            combine(0)

        @pl.loop(1, 4)
        def _(i):
            p = row + (i % 2) * (2 - 4 * x) + (i // 2) * (4 - 8 * y)
            put(G.at[h, p], G.at[h, p], a_s.at[h, 3 + i], a_r.at[h, 3 + i], (sib, z)).wait_recv()
            add_chip(h, p // 2)

        for n in ((0,), (1, 2))[h]:
            b_send(n)

    @pl.loop(0, secs)
    def _(s):
        tt = [T[s, t].T for t in range(T.shape[1])]
        rows = pl.ds(pl.multiple_of(((s % 2) * chips + s // 2) * blk, blk), blk)
        for k in range(reps):
            m = masks(s, k)
            val = tt[0] * m[0]
            for t in range(1, T.shape[1]):
                val = val + tt[t] * m[t]
            hi, lo = split(val)
            AThi[rows, k * blk:(k + 1) * blk] = hi
            ATlo[rows, k * blk:(k + 1) * blk] = lo

    combine(1)
    combine(2)
    loads[3].wait()
    loads[4].wait()

    def d_put(n, k, slot, dev):
        h, at, size = d_pc[n]
        ref = Bk.at[h, k, at:at + size]
        return put(ref, ref, d_s.at[n, slot], d_r.at[n, slot], (row, dev))

    def d_send(n):
        @pl.when(inner)
        def _():
            d_put(n, z, 2, mir).start()

        d_put(n, z, 0, near).start()

    w = W[...]
    agg0 = b_sum(0)
    pre0 = mm3(agg0, w[:blk])
    agg1, delta = [], []
    for n in (1, 2):
        at = b_pc[n][1]
        agg1.append(b_sum(n))
        pre = pre0[at:at + rh] + mm3(agg1[-1], w[blk:])
        sig = 1.0 / (1.0 + jnp.exp(-pre))
        delta.append(C[at:at + rh] * (sig * (1.0 + pre * (1.0 - sig))))
        back = mm3(delta[-1], w, ((1,), (1,)))
        for h in range(2):
            Bk[h, z, at:at + rh] = back[:, h * blk:(h + 1) * blk]
        d_send(n - 1)
        Ho[at:at + rh] = pre * sig
    d_send(2)
    agg = jnp.concatenate([agg0, jnp.concatenate(agg1, axis=0)], axis=1)
    delta = jnp.concatenate(delta, axis=0)
    hid_cp = pltpu.make_async_copy(Ho, hid_o, loc_sem.at[5])
    hid_cp.start()

    def relay(n):
        @pl.when(inner)
        def _():
            d_put(n, mir, 2, mir).wait_recv()
            d_put(n, mir, 1, near).start()

        @pl.when(outer)
        def _():
            d_put(n, near, 0, near).wait_recv()
            d_put(n, z, 2, mir).start()
            d_put(n, z, 1, far).start()


    wt[...] = mm3(agg.T, delta) * (1.0 / math.sqrt(blk * secs * reps))
    half = wt.shape[0] // 2
    piece = half // chips
    sub = piece // reps
    oth = pl.multiple_of((1 - c) * half, half)
    own = pl.multiple_of(c * half, half)
    g1 = send(wt.at[pl.ds(oth, half)], ws, g_s.at[0], g_r.at[0], (sib, z))
    relay(0)
    relay(1)
    drain()
    for n in range(3):
        for i in range(3):
            b_put(n, z, i, near).wait_send()
    g1.wait_recv()
    wc[...] = wt[pl.ds(own, half)] + ws[...]
    g2 = [send(wc.at[pl.ds(pl.multiple_of((p // 2) * piece, piece), piece)], wr.at[i], g_s.at[1 + i], g_r.at[1 + i], (p, z))
          for i, p in enumerate(plane)]

    def rows_start(h):
        parts = ((0, 1 - c), (1, c))
        at = [pl.ds(pl.multiple_of(core * (chips * blk), chips * blk), chips * blk) for _, core in parts]

        def pair(k):
            cols = pl.ds(pl.multiple_of(k * blk, 2 * blk), 2 * blk)
            rhs = pair_rhs(Bk[h, pl.ds(k, 2)])
            return [lambda a=a: pair_mm(AThi[a, cols], ATlo[a, cols], rhs).reshape(chips, blk, blk) for a in at]

        pieces = ((0, 1), (2,))[h]

        @pl.when(inner)
        def _():
            for n in pieces:
                d_put(n, near, 0, near).wait_recv()

        here = (z // 2) * 2
        for i, part in enumerate(pair(here)):
            Rs[h, i] = part()
        for n in pieces:
            d_put(n, far, 1, far).wait_recv()

        @pl.when(outer)
        def _():
            for n in pieces:
                d_put(n, mir, 2, mir).wait_recv()

        out = []
        for i, part in enumerate(pair(2 - here)):
            Rs[h, i] = Rs[h, i] + part()
            if i == 0:
                out = [send(Rs.at[h, 0, p // 2], Es.at[h, p // 2], e_s.at[h, 3 + m], e_r.at[h, 3 + m], (sib, z))
                       for m, p in enumerate((dg, xn, yn, row))]
        return out

    def rows_mid(h, cps):
        out = []
        for i, p in enumerate((dg, xn, yn)):
            cps[i].wait_recv()
            Ec[h, i] = Rs[h, 1, p // 2] + Es[h, p // 2]
            out.append(send(Ec.at[h, i], Er.at[h, i], e_s.at[h, i], e_r.at[h, i], (p, z)))
        cps[3].wait_recv()
        return out

    def rows_end(h, cps):
        total = Rs[h, 1, q] + Es[h, q]
        for i, cp in enumerate(cps):
            cp.wait_recv()
            total = total + Er[h, i]
        Fo[:, h * blk:(h + 1) * blk] = total

    relay(2)
    e0 = rows_start(0)
    e0 = rows_mid(0, e0)

    at = pl.multiple_of(q * piece, piece)
    total = wc[pl.ds(at, piece)]
    for i in range(3):
        g2[i].wait_recv()
        total = total + wr[i]
    wz[...] = total
    g3 = [send(wz.at[pl.ds(pl.multiple_of(k * sub, sub), sub)], wzr.at[i], g_s.at[4 + i], g_r.at[4 + i], (row, k))
          for i, k in enumerate(zs)]

    total = wz[pl.ds(pl.multiple_of(z * sub, sub), sub)]
    for i in range(reps - 1):
        g3[i].wait_recv()
        total = total + wzr[i]
    top = c * half + q * piece
    mine = pl.ds(pl.multiple_of(top + z * sub, sub), sub)
    gw[mine] = total
    g4 = [send(gw.at[mine], gw.at[mine], g_s.at[7 + i], g_r.at[7 + i], (row, k)) for i, k in enumerate(zs)]
    e1 = rows_start(1)
    for cp in g4:
        cp.wait_recv()
    mine = pl.ds(pl.multiple_of(top, piece), piece)
    g5 = [send(gw.at[mine], gw.at[mine], g_s.at[10 + i], g_r.at[10 + i], (p, z)) for i, p in enumerate(plane)]

    e1 = rows_mid(1, e1)
    rows_end(0, e0)

    for cp in g5:
        cp.wait_recv()
    mine = pl.ds(own, half)
    g6 = send(gw.at[mine], gw.at[mine], g_s.at[13], g_r.at[13], (sib, z))

    rows_end(1, e1)
    f_cp = pltpu.make_async_copy(Fo, gf_o, loc_sem.at[6])
    f_cp.start()
    g6.wait_recv()
    g_cp = pltpu.make_async_copy(gw, gw_o, loc_sem.at[7])
    g_cp.start()
    drain()
    for n in range(3):
        for i in range(3):
            d_put(n, z, i, near).wait_send()
    hid_cp.wait()
    f_cp.wait()
    g_cp.wait()


def store(a, b, c, x, y, z, u, v, w, sem):
    bufs = ((a, u, x), (b, v, y), (c, w, z))
    ins = [pltpu.make_async_copy(s, t, sem.at[0, i]) for i, (s, t, _) in enumerate(bufs)]
    outs = [pltpu.make_async_copy(t, d, sem.at[1, i]) for i, (_, t, d) in enumerate(bufs)]
    for cp in ins:
        cp.start()
    for cp, out in zip(ins, outs):
        cp.wait()
        out.start()
    for out in outs:
        out.wait()


def fused(features, weight, cotangent, tiles, tile_count, tile_block):
    blk, width = features.shape
    secs, slots = tiles.shape[2], tiles.shape[3]
    reps = lax.axis_size("rep")
    chips = secs // 2
    half = width // 2
    piece = half // chips
    sub = piece // reps
    V = pltpu.VMEM
    dma = pltpu.SemaphoreType.DMA
    hbm = pl.BlockSpec(memory_space=pltpu.HBM)
    smem = pl.BlockSpec(memory_space=pltpu.SMEM)
    flops = 2 * 3 * 2 * (reps * blk) * (secs * blk) * width
    raw = pl.pallas_call(
        kernel,
        out_shape=(jax.ShapeDtypeStruct((blk, width), F32), jax.ShapeDtypeStruct((width, width), F32),
                   jax.ShapeDtypeStruct((blk, width), F32)),
        in_specs=[hbm, hbm, hbm, hbm, smem, smem],
        out_specs=(hbm,) * 3,
        scratch_shapes=[
            V((2, secs, blk, blk), F32), V((secs, slots, blk, blk), F32), V((width, width), F32), V((blk, width), F32),
            V((reps * blk, secs * blk), BF16), V((reps * blk, secs * blk), BF16),
            V((secs * blk, reps * blk), BF16), V((secs * blk, reps * blk), BF16),
            V((2, reps, blk, blk), F32), V((2, reps - 1, blk, blk), F32), V((2, blk, blk), F32), V((2, reps, blk, blk), F32),
            V((2, 2, chips, blk, blk), F32), V((2, chips, blk, blk), F32), V((2, 3, blk, blk), F32), V((2, 3, blk, blk), F32),
            V((blk, width), F32), V((blk, width), F32),
            V((width, width), F32), V((half, width), F32), V((half, width), F32), V((3, piece, width), F32),
            V((piece, width), F32), V((reps - 1, sub, width), F32), V((width, width), F32),
            dma((8,)), dma((2, 7)), dma((2, 7)), dma((3, 3)), dma((3, 3)), dma((3,)), dma((3, 3)), dma((3, 3)),
            dma((2, 7)), dma((2, 7)), dma((14,)), dma((14,)),
        ],
        compiler_params=pltpu.CompilerParams(collective_id=0, has_side_effects=True, vmem_limit_bytes=LIMIT),
        cost_estimate=pl.CostEstimate(flops=flops, bytes_accessed=4 * tiles.size, transcendentals=blk * width),
        name="graph_step",
    )(features, weight, cotangent, tiles, tile_count, tile_block.transpose(0, 1, 3, 2))
    return pl.pallas_call(
        store,
        out_shape=tuple(jax.ShapeDtypeStruct(r.shape, r.dtype) for r in raw),
        in_specs=[hbm] * 3,
        out_specs=(hbm,) * 3,
        scratch_shapes=[V(r.shape, r.dtype) for r in raw] + [dma((2, 3))],
        compiler_params=pltpu.CompilerParams(vmem_limit_bytes=LIMIT),
        name="store_results",
    )(*raw)


def silu_slope(pre):
    sig = jax.nn.sigmoid(pre)
    return sig * (1.0 + pre * (1.0 - sig))


def body(features, weight, cotangent, tiles, tile_count, tile_block):
    highest = lax.Precision.HIGHEST
    tile_set = tiles[0, 0]
    counts = tile_count[0, 0]
    block_ids = tile_block[0, 0]
    sections = tile_set.shape[0]
    slots = tile_set.shape[1]
    blk = tile_set.shape[2]
    width = features.shape[1]
    groups = lax.axis_size("rep")
    select = (
        (block_ids[..., None] == jnp.arange(groups, dtype=jnp.int32))
        & (jnp.arange(slots, dtype=jnp.int32)[:, None] < counts[:, None, None])
    ).astype(jnp.float32)
    gathered = lax.all_gather(features, "rows", axis=0, tiled=True).reshape(sections, blk, width)
    prods = jnp.einsum("stab,sbf->staf", tile_set, gathered, precision=highest)
    total = jnp.einsum("stk,staf->kaf", select, prods, precision=highest)
    aggregated = lax.psum_scatter(
        total.reshape(groups * blk, width), "rep", scatter_dimension=0, tiled=True
    )
    pre = jnp.dot(aggregated, weight, precision=highest)
    hidden = jax.nn.silu(pre)
    delta = cotangent * silu_slope(pre)
    weight_term = jnp.dot(aggregated.T, delta, precision=highest)
    node_total = blk * lax.axis_size("rows") * groups
    grad_weight = lax.psum(weight_term, ("rows", "rep")) / math.sqrt(node_total)
    back = jnp.dot(delta, weight.T, precision=highest)
    group_back = lax.all_gather(back, "rep", axis=0, tiled=True).reshape(groups, blk, width)
    count = sections * blk
    picked = jnp.einsum("stk,kaf->staf", select, group_back, precision=highest)
    result = jnp.einsum("stab,staf->sbf", tile_set, picked, precision=highest)
    all_terms = result.reshape(count, width)
    grad_features = lax.psum_scatter(all_terms, "rows", scatter_dimension=0, tiled=True)
    return (hidden, grad_weight, grad_features)


def solution(mesh):
    in_specs = (
        P(("rows", "rep"), None),
        P(),
        P(("rows", "rep"), None),
        P("rows", "rep", None, None, None, None),
        P("rows", "rep", None),
        P("rows", "rep", None, None),
    )
    out_specs = (P(("rows", "rep"), None), P(), P(("rows", "rep"), None))
    fits = mesh.shape["rows"] == 8 and mesh.shape["rep"] == 4
    return jax.shard_map(fused if fits else body, mesh=mesh, in_specs=in_specs, out_specs=out_specs, check_vma=False)
```

```python
import functools
import math

import jax
import jax.numpy as jnp
from jax import lax
from jax.experimental import pallas as pl
from jax.experimental.pallas import tpu as pltpu
from jax.sharding import PartitionSpec as P

LIMIT = 60 * 1024 * 1024
MESH = pl.DeviceIdType.MESH
F32 = jnp.float32
BF16 = jnp.bfloat16


def split(x):
    hi = x.astype(BF16)
    return hi, (x - hi.astype(F32)).astype(BF16)


def mm(a, b, dims=((1,), (0,))):
    return lax.dot_general(a, b, (dims, ((), ())), preferred_element_type=F32)


def mm3(a, b, dims=((1,), (0,))):
    (ah, al), (bh, bl) = split(a), split(b)
    return mm(ah, bh, dims) + (mm(ah, bl, dims) + mm(al, bh, dims))


def kernel(feat, weight, cot, tiles, cnt, blks, hid_o, gw_o, gf_o,
           G, T, W, C, Ahi, Alo, AThi, ATlo, Pb, Rb, St, Bk, Rs, Es, Ec, Er, Ho, Fo,
           wt, ws, wc, wr, wz, wzr, gw,
           loc_sem, a_s, a_r, b_s, b_r, st_r, d_s, d_r, e_s, e_r, g_s, g_r):
    blk = T.shape[2]
    secs = T.shape[0]
    reps = Pb.shape[1]
    chips = secs // 2
    quarter = reps * blk
    row = lax.axis_index("rows")
    z = lax.axis_index("rep")
    c = row % 2
    q = row // 2
    x = q % 2
    y = q // 2
    sib = row + 1 - 2 * c
    xn = row + 2 - 4 * x
    yn = row + 4 - 8 * y
    dg = xn + yn - row
    plane = (dg, xn, yn)
    zs = [(z + d) % reps for d in range(1, reps)]
    near = z + 1 - 2 * (z % 2)
    far = (z + 2) % reps
    mir = reps - 1 - z
    inner = (z == 1) | (z == 2)
    outer = (z == 0) | (z == 3)

    barrier = pltpu.get_barrier_semaphore()
    peers = [(sib, z)] + [(p, z) for p in plane] + [(row, k) for k in zs]
    for dev in peers:
        pl.semaphore_signal(barrier, inc=1, device_id=dev, device_id_type=MESH)
    loads = [pltpu.make_async_copy(feat.at[:, h * blk:(h + 1) * blk], G.at[h, row], loc_sem.at[h]) for h in range(2)]
    loads += [pltpu.make_async_copy(tiles.at[0, 0], T, loc_sem.at[2]),
              pltpu.make_async_copy(weight, W, loc_sem.at[3]),
              pltpu.make_async_copy(cot, C, loc_sem.at[4])]
    for ld in loads:
        ld.start()
    pl.semaphore_wait(barrier, len(peers))

    sent = []

    def put(src, dst, ss, rs, dev):
        return pltpu.make_async_remote_copy(src_ref=src, dst_ref=dst, send_sem=ss, recv_sem=rs,
                                            device_id=dev, device_id_type=MESH)

    def send(src, dst, ss, rs, dev):
        cp = pltpu.make_async_remote_copy(src_ref=src, dst_ref=dst, send_sem=ss, recv_sem=rs,
                                          device_id=dev, device_id_type=MESH)
        cp.start()
        sent.append(cp)
        return cp

    def drain():
        while sent:
            sent.pop(0).wait_send()

    a_cp = []

    def gather(h):
        loads[h].wait()
        mine = G.at[h, row]
        a_cp.append([send(mine, mine, a_s.at[h, i], a_r.at[h, i], (p, z)) for i, p in ((3, dg), (1, xn), (2, yn), (0, sib))])

    gather(0)

    loads[2].wait()

    def masks(s, k):
        n = cnt[0, 0, s]
        return [jnp.where((blks[0, 0, t, s] == k) & (t < n), 1.0, 0.0).astype(F32) for t in range(T.shape[1])]

    @pl.loop(0, secs)
    def _(s):
        for k in range(reps):
            m = masks(s, k)
            val = T[s, 0] * m[0]
            for t in range(1, T.shape[1]):
                val = val + T[s, t] * m[t]
            hi, lo = split(val)
            cols = pl.ds(pl.multiple_of(s * blk, blk), blk)
            Ahi[k * blk:(k + 1) * blk, cols] = hi
            Alo[k * blk:(k + 1) * blk, cols] = lo

    rh = blk // 2
    b_pc = ((0, 0, blk), (1, 0, rh), (1, rh, rh))
    d_pc = ((0, 0, rh), (0, rh, rh), (1, 0, blk))

    def b_put(n, k, slot, dev):
        h, at, size = b_pc[n]
        return put(Pb.at[h, k, at:at + size], Rb.at[h, slot, at:at + size], b_s.at[n, slot], b_r.at[n, slot], (row, dev))

    def stage_put(n):
        h, at, size = b_pc[n]
        return put(Pb.at[h, mir, at:at + size], St.at[h, at:at + size], b_s.at[n, 2], st_r.at[n], (row, near))

    def b_send(n):
        @pl.when(outer)
        def _():
            stage_put(n).start()
            b_put(n, far, 1, far).start()
            b_put(n, near, 0, near).start()

        @pl.when(inner)
        def _():
            b_put(n, mir, 2, mir).start()
            b_put(n, near, 0, near).start()

    def combine(n):
        h, at, size = b_pc[n]

        @pl.when(inner)
        def _():
            stage_put(n).wait_recv()
            Pb[h, far, at:at + size] = Pb[h, far, at:at + size] + St[h, at:at + size]
            b_put(n, far, 1, far).start()

    def b_sum(n):
        h, at, size = b_pc[n]
        b_put(n, near, 0, near).wait_recv()
        part = Pb[h, z, at:at + size] + Rb[h, 0, at:at + size]

        @pl.when(inner)
        def _():
            b_put(n, mir, 2, mir).wait_recv()

        @pl.when(outer)
        def _():
            Rb[h, 2, at:at + size] = jnp.zeros((size, blk), F32)

        part = part + Rb[h, 2, at:at + size]
        b_put(n, far, 1, far).wait_recv()
        return part + Rb[h, 1, at:at + size]

    def pair_rhs(ref):
        hi, lo = split(ref.reshape(2 * blk, blk))
        return jnp.concatenate([hi, lo], axis=1)

    def pair_mm(ah, al, rhs):
        acc = mm(ah, rhs)
        return acc[:, :blk] + (acc[:, blk:] + mm(al, rhs[:, :blk]))

    def add_chip(h, chip, first=False):
        cols = pl.ds(pl.multiple_of(chip * (2 * blk), 2 * blk), 2 * blk)
        part = pair_mm(Ahi[:, cols], Alo[:, cols], pair_rhs(G[h, pl.ds(2 * chip, 2)])).reshape(reps, blk, blk)
        Pb[h] = part if first else Pb[h] + part

    for h in range(2):

        def forward(i, p):
            put(G.at[h, p], G.at[h, p], a_s.at[h, i], a_r.at[h, i], (p, z)).wait_recv()
            send(G.at[h, p], G.at[h, p], a_s.at[h, 3 + i], a_r.at[h, 3 + i], (sib, z))

        forward(1, xn)
        forward(2, yn)
        a_cp[h][3].wait_recv()
        add_chip(h, q, True)
        forward(3, dg)
        if h == 0:
            gather(1)
        else:
            combine(0)

        @pl.loop(1, 4)
        def _(i):
            p = row + (i % 2) * (2 - 4 * x) + (i // 2) * (4 - 8 * y)
            put(G.at[h, p], G.at[h, p], a_s.at[h, 3 + i], a_r.at[h, 3 + i], (sib, z)).wait_recv()
            add_chip(h, p // 2)

        for n in ((0,), (1, 2))[h]:
            b_send(n)

    @pl.loop(0, secs)
    def _(s):
        tt = [T[s, t].T for t in range(T.shape[1])]
        rows = pl.ds(pl.multiple_of(((s % 2) * chips + s // 2) * blk, blk), blk)
        for k in range(reps):
            m = masks(s, k)
            val = tt[0] * m[0]
            for t in range(1, T.shape[1]):
                val = val + tt[t] * m[t]
            hi, lo = split(val)
            AThi[rows, k * blk:(k + 1) * blk] = hi
            ATlo[rows, k * blk:(k + 1) * blk] = lo

    combine(1)
    combine(2)
    loads[3].wait()
    loads[4].wait()

    def d_put(n, k, slot, dev):
        h, at, size = d_pc[n]
        ref = Bk.at[h, k, at:at + size]
        return put(ref, ref, d_s.at[n, slot], d_r.at[n, slot], (row, dev))

    def d_send(n):
        d_put(n, z, 2, mir).start()

        @pl.when(outer)
        def _():
            d_put(n, z, 1, far).start()

        d_put(n, z, 0, near).start()

    w = W[...]
    agg0 = b_sum(0)
    pre0 = mm3(agg0, w[:blk])
    agg1, delta = [], []
    for n in (1, 2):
        at = b_pc[n][1]
        agg1.append(b_sum(n))
        pre = pre0[at:at + rh] + mm3(agg1[-1], w[blk:])
        sig = 1.0 / (1.0 + jnp.exp(-pre))
        delta.append(C[at:at + rh] * (sig * (1.0 + pre * (1.0 - sig))))
        back = mm3(delta[-1], w, ((1,), (1,)))
        for h in range(2):
            Bk[h, z, at:at + rh] = back[:, h * blk:(h + 1) * blk]
        d_send(n - 1)
        Ho[at:at + rh] = pre * sig
    d_send(2)
    agg = jnp.concatenate([agg0, jnp.concatenate(agg1, axis=0)], axis=1)
    delta = jnp.concatenate(delta, axis=0)
    hid_cp = pltpu.make_async_copy(Ho, hid_o, loc_sem.at[5])
    hid_cp.start()

    def relay(n):
        @pl.when(inner)
        def _():
            d_put(n, mir, 2, mir).wait_recv()
            d_put(n, mir, 1, near).start()


    wt[...] = mm3(agg.T, delta) * (1.0 / math.sqrt(blk * secs * reps))
    half = wt.shape[0] // 2
    piece = half // chips
    sub = piece // reps
    oth = pl.multiple_of((1 - c) * half, half)
    own = pl.multiple_of(c * half, half)
    g1 = send(wt.at[pl.ds(oth, half)], ws, g_s.at[0], g_r.at[0], (sib, z))
    relay(0)
    relay(1)
    drain()
    for n in range(3):
        for i in range(3):
            b_put(n, z, i, near).wait_send()
    g1.wait_recv()
    wc[...] = wt[pl.ds(own, half)] + ws[...]
    g2 = [send(wc.at[pl.ds(pl.multiple_of((p // 2) * piece, piece), piece)], wr.at[i], g_s.at[1 + i], g_r.at[1 + i], (p, z))
          for i, p in enumerate(plane)]

    def rows_start(h):
        parts = ((0, 1 - c), (1, c))
        at = [pl.ds(pl.multiple_of(core * (chips * blk), chips * blk), chips * blk) for _, core in parts]

        def pair(k):
            cols = pl.ds(pl.multiple_of(k * blk, 2 * blk), 2 * blk)
            rhs = pair_rhs(Bk[h, pl.ds(k, 2)])
            return [lambda a=a: pair_mm(AThi[a, cols], ATlo[a, cols], rhs).reshape(chips, blk, blk) for a in at]

        pieces = ((0, 1), (2,))[h]
        for n in pieces:
            d_put(n, near, 0, near).wait_recv()
        here = (z // 2) * 2
        for i, part in enumerate(pair(here)):
            Rs[h, i] = part()
        for n in pieces:
            d_put(n, far, 1, far).wait_recv()

        @pl.when(outer)
        def _():
            for n in pieces:
                d_put(n, mir, 2, mir).wait_recv()

        out = []
        for i, part in enumerate(pair(2 - here)):
            Rs[h, i] = Rs[h, i] + part()
            if i == 0:
                out = [send(Rs.at[h, 0, p // 2], Es.at[h, p // 2], e_s.at[h, 3 + m], e_r.at[h, 3 + m], (sib, z))
                       for m, p in enumerate((dg, xn, yn, row))]
        return out

    def rows_mid(h, cps):
        out = []
        for i, p in enumerate((dg, xn, yn)):
            cps[i].wait_recv()
            Ec[h, i] = Rs[h, 1, p // 2] + Es[h, p // 2]
            out.append(send(Ec.at[h, i], Er.at[h, i], e_s.at[h, i], e_r.at[h, i], (p, z)))
        cps[3].wait_recv()
        return out

    def rows_end(h, cps):
        total = Rs[h, 1, q] + Es[h, q]
        for i, cp in enumerate(cps):
            cp.wait_recv()
            total = total + Er[h, i]
        Fo[:, h * blk:(h + 1) * blk] = total

    e0 = rows_start(0)
    relay(2)
    e0 = rows_mid(0, e0)

    at = pl.multiple_of(q * piece, piece)
    total = wc[pl.ds(at, piece)]
    for i in range(3):
        g2[i].wait_recv()
        total = total + wr[i]
    wz[...] = total
    g3 = [send(wz.at[pl.ds(pl.multiple_of(k * sub, sub), sub)], wzr.at[i], g_s.at[4 + i], g_r.at[4 + i], (row, k))
          for i, k in enumerate(zs)]

    total = wz[pl.ds(pl.multiple_of(z * sub, sub), sub)]
    for i in range(reps - 1):
        g3[i].wait_recv()
        total = total + wzr[i]
    top = c * half + q * piece
    mine = pl.ds(pl.multiple_of(top + z * sub, sub), sub)
    gw[mine] = total
    g4 = [send(gw.at[mine], gw.at[mine], g_s.at[7 + i], g_r.at[7 + i], (row, k)) for i, k in enumerate(zs)]
    e1 = rows_start(1)
    for cp in g4:
        cp.wait_recv()
    mine = pl.ds(pl.multiple_of(top, piece), piece)
    g5 = [send(gw.at[mine], gw.at[mine], g_s.at[10 + i], g_r.at[10 + i], (p, z)) for i, p in enumerate(plane)]

    e1 = rows_mid(1, e1)
    rows_end(0, e0)

    for cp in g5:
        cp.wait_recv()
    mine = pl.ds(own, half)
    g6 = send(gw.at[mine], gw.at[mine], g_s.at[13], g_r.at[13], (sib, z))

    rows_end(1, e1)
    f_cp = pltpu.make_async_copy(Fo, gf_o, loc_sem.at[6])
    f_cp.start()
    g6.wait_recv()
    g_cp = pltpu.make_async_copy(gw, gw_o, loc_sem.at[7])
    g_cp.start()
    drain()
    for n in range(3):
        for i in range(3):
            d_put(n, z, i, near).wait_send()
    hid_cp.wait()
    f_cp.wait()
    g_cp.wait()


def store(a, b, c, x, y, z, u, v, w, sem):
    bufs = ((a, u, x), (b, v, y), (c, w, z))
    ins = [pltpu.make_async_copy(s, t, sem.at[0, i]) for i, (s, t, _) in enumerate(bufs)]
    outs = [pltpu.make_async_copy(t, d, sem.at[1, i]) for i, (_, t, d) in enumerate(bufs)]
    for cp in ins:
        cp.start()
    for cp, out in zip(ins, outs):
        cp.wait()
        out.start()
    for out in outs:
        out.wait()


def fused(features, weight, cotangent, tiles, tile_count, tile_block):
    blk, width = features.shape
    secs, slots = tiles.shape[2], tiles.shape[3]
    reps = lax.axis_size("rep")
    chips = secs // 2
    half = width // 2
    piece = half // chips
    sub = piece // reps
    V = pltpu.VMEM
    dma = pltpu.SemaphoreType.DMA
    hbm = pl.BlockSpec(memory_space=pltpu.HBM)
    smem = pl.BlockSpec(memory_space=pltpu.SMEM)
    flops = 2 * 3 * 2 * (reps * blk) * (secs * blk) * width
    raw = pl.pallas_call(
        kernel,
        out_shape=(jax.ShapeDtypeStruct((blk, width), F32), jax.ShapeDtypeStruct((width, width), F32),
                   jax.ShapeDtypeStruct((blk, width), F32)),
        in_specs=[hbm, hbm, hbm, hbm, smem, smem],
        out_specs=(hbm,) * 3,
        scratch_shapes=[
            V((2, secs, blk, blk), F32), V((secs, slots, blk, blk), F32), V((width, width), F32), V((blk, width), F32),
            V((reps * blk, secs * blk), BF16), V((reps * blk, secs * blk), BF16),
            V((secs * blk, reps * blk), BF16), V((secs * blk, reps * blk), BF16),
            V((2, reps, blk, blk), F32), V((2, reps - 1, blk, blk), F32), V((2, blk, blk), F32), V((2, reps, blk, blk), F32),
            V((2, 2, chips, blk, blk), F32), V((2, chips, blk, blk), F32), V((2, 3, blk, blk), F32), V((2, 3, blk, blk), F32),
            V((blk, width), F32), V((blk, width), F32),
            V((width, width), F32), V((half, width), F32), V((half, width), F32), V((3, piece, width), F32),
            V((piece, width), F32), V((reps - 1, sub, width), F32), V((width, width), F32),
            dma((8,)), dma((2, 7)), dma((2, 7)), dma((3, 3)), dma((3, 3)), dma((3,)), dma((3, 3)), dma((3, 3)),
            dma((2, 7)), dma((2, 7)), dma((14,)), dma((14,)),
        ],
        compiler_params=pltpu.CompilerParams(collective_id=0, has_side_effects=True, vmem_limit_bytes=LIMIT),
        cost_estimate=pl.CostEstimate(flops=flops, bytes_accessed=4 * tiles.size, transcendentals=blk * width),
        name="graph_step",
    )(features, weight, cotangent, tiles, tile_count, tile_block.transpose(0, 1, 3, 2))
    return pl.pallas_call(
        store,
        out_shape=tuple(jax.ShapeDtypeStruct(r.shape, r.dtype) for r in raw),
        in_specs=[hbm] * 3,
        out_specs=(hbm,) * 3,
        scratch_shapes=[V(r.shape, r.dtype) for r in raw] + [dma((2, 3))],
        compiler_params=pltpu.CompilerParams(vmem_limit_bytes=LIMIT),
        name="store_results",
    )(*raw)


def silu_slope(pre):
    sig = jax.nn.sigmoid(pre)
    return sig * (1.0 + pre * (1.0 - sig))


def body(features, weight, cotangent, tiles, tile_count, tile_block):
    highest = lax.Precision.HIGHEST
    tile_set = tiles[0, 0]
    counts = tile_count[0, 0]
    block_ids = tile_block[0, 0]
    sections = tile_set.shape[0]
    slots = tile_set.shape[1]
    blk = tile_set.shape[2]
    width = features.shape[1]
    groups = lax.axis_size("rep")
    select = (
        (block_ids[..., None] == jnp.arange(groups, dtype=jnp.int32))
        & (jnp.arange(slots, dtype=jnp.int32)[:, None] < counts[:, None, None])
    ).astype(jnp.float32)
    gathered = lax.all_gather(features, "rows", axis=0, tiled=True).reshape(sections, blk, width)
    prods = jnp.einsum("stab,sbf->staf", tile_set, gathered, precision=highest)
    total = jnp.einsum("stk,staf->kaf", select, prods, precision=highest)
    aggregated = lax.psum_scatter(
        total.reshape(groups * blk, width), "rep", scatter_dimension=0, tiled=True
    )
    pre = jnp.dot(aggregated, weight, precision=highest)
    hidden = jax.nn.silu(pre)
    delta = cotangent * silu_slope(pre)
    weight_term = jnp.dot(aggregated.T, delta, precision=highest)
    node_total = blk * lax.axis_size("rows") * groups
    grad_weight = lax.psum(weight_term, ("rows", "rep")) / math.sqrt(node_total)
    back = jnp.dot(delta, weight.T, precision=highest)
    group_back = lax.all_gather(back, "rep", axis=0, tiled=True).reshape(groups, blk, width)
    count = sections * blk
    picked = jnp.einsum("stk,kaf->staf", select, group_back, precision=highest)
    result = jnp.einsum("stab,staf->sbf", tile_set, picked, precision=highest)
    all_terms = result.reshape(count, width)
    grad_features = lax.psum_scatter(all_terms, "rows", scatter_dimension=0, tiled=True)
    return (hidden, grad_weight, grad_features)


def solution(mesh):
    in_specs = (
        P(("rows", "rep"), None),
        P(),
        P(("rows", "rep"), None),
        P("rows", "rep", None, None, None, None),
        P("rows", "rep", None),
        P("rows", "rep", None, None),
    )
    out_specs = (P(("rows", "rep"), None), P(), P(("rows", "rep"), None))
    fits = mesh.shape["rows"] == 8 and mesh.shape["rep"] == 4
    return jax.shard_map(fused if fits else body, mesh=mesh, in_specs=in_specs, out_specs=out_specs, check_vma=False)
```

```python
import functools
import math

import jax
import jax.numpy as jnp
from jax import lax
from jax.experimental import pallas as pl
from jax.experimental.pallas import tpu as pltpu
from jax.sharding import PartitionSpec as P

LIMIT = 60 * 1024 * 1024
MESH = pl.DeviceIdType.MESH
F32 = jnp.float32
BF16 = jnp.bfloat16


def split(x):
    hi = x.astype(BF16)
    return hi, (x - hi.astype(F32)).astype(BF16)


def mm(a, b, dims=((1,), (0,))):
    return lax.dot_general(a, b, (dims, ((), ())), preferred_element_type=F32)


def mm3(a, b, dims=((1,), (0,))):
    (ah, al), (bh, bl) = split(a), split(b)
    return mm(ah, bh, dims) + (mm(ah, bl, dims) + mm(al, bh, dims))


def kernel(feat, weight, cot, tiles, cnt, blks, hid_o, gw_o, gf_o,
           G, T, W, C, Ahi, Alo, AThi, ATlo, Pb, Rb, St, Bk, Rs, Es, Ec, Er, Ho, Fo,
           wt, ws, wc, wr, wz, wzr, gw,
           loc_sem, a_s, a_r, b_s, b_r, st_r, d_s, d_r, e_s, e_r, g_s, g_r):
    blk = T.shape[2]
    secs = T.shape[0]
    reps = Pb.shape[1]
    chips = secs // 2
    quarter = reps * blk
    row = lax.axis_index("rows")
    z = lax.axis_index("rep")
    c = row % 2
    q = row // 2
    x = q % 2
    y = q // 2
    sib = row + 1 - 2 * c
    xn = row + 2 - 4 * x
    yn = row + 4 - 8 * y
    dg = xn + yn - row
    plane = (dg, xn, yn)
    zs = [(z + d) % reps for d in range(1, reps)]
    near = z + 1 - 2 * (z % 2)
    far = (z + 2) % reps
    mir = reps - 1 - z
    inner = (z == 1) | (z == 2)
    outer = (z == 0) | (z == 3)

    barrier = pltpu.get_barrier_semaphore()
    peers = [(sib, z)] + [(p, z) for p in plane] + [(row, k) for k in zs]
    for dev in peers:
        pl.semaphore_signal(barrier, inc=1, device_id=dev, device_id_type=MESH)
    loads = [pltpu.make_async_copy(feat.at[:, h * blk:(h + 1) * blk], G.at[h, row], loc_sem.at[h]) for h in range(2)]
    loads += [pltpu.make_async_copy(tiles.at[0, 0], T, loc_sem.at[2]),
              pltpu.make_async_copy(weight, W, loc_sem.at[3]),
              pltpu.make_async_copy(cot, C, loc_sem.at[4])]
    for ld in loads:
        ld.start()
    pl.semaphore_wait(barrier, len(peers))

    sent = []

    def put(src, dst, ss, rs, dev):
        return pltpu.make_async_remote_copy(src_ref=src, dst_ref=dst, send_sem=ss, recv_sem=rs,
                                            device_id=dev, device_id_type=MESH)

    def send(src, dst, ss, rs, dev):
        cp = pltpu.make_async_remote_copy(src_ref=src, dst_ref=dst, send_sem=ss, recv_sem=rs,
                                          device_id=dev, device_id_type=MESH)
        cp.start()
        sent.append(cp)
        return cp

    def drain():
        while sent:
            sent.pop(0).wait_send()

    a_cp = []

    def gather(h):
        loads[h].wait()
        mine = G.at[h, row]
        a_cp.append([send(mine, mine, a_s.at[h, i], a_r.at[h, i], (p, z)) for i, p in ((3, dg), (1, xn), (2, yn), (0, sib))])

    gather(0)

    loads[2].wait()

    def masks(s, k):
        n = cnt[0, 0, s]
        return [jnp.where((blks[0, 0, t, s] == k) & (t < n), 1.0, 0.0).astype(F32) for t in range(T.shape[1])]

    @pl.loop(0, secs)
    def _(s):
        for k in range(reps):
            m = masks(s, k)
            val = T[s, 0] * m[0]
            for t in range(1, T.shape[1]):
                val = val + T[s, t] * m[t]
            hi, lo = split(val)
            cols = pl.ds(pl.multiple_of(s * blk, blk), blk)
            Ahi[k * blk:(k + 1) * blk, cols] = hi
            Alo[k * blk:(k + 1) * blk, cols] = lo

    rh = blk // 2
    b_pc = ((0, 0, blk), (1, 0, rh), (1, rh, rh))
    d_pc = ((0, 0, rh), (0, rh, rh), (1, 0, blk))

    def b_put(n, k, slot, dev):
        h, at, size = b_pc[n]
        return put(Pb.at[h, k, at:at + size], Rb.at[h, slot, at:at + size], b_s.at[n, slot], b_r.at[n, slot], (row, dev))

    def stage_put(n):
        h, at, size = b_pc[n]
        return put(Pb.at[h, mir, at:at + size], St.at[h, at:at + size], b_s.at[n, 2], st_r.at[n], (row, near))

    def b_send(n):
        @pl.when(outer)
        def _():
            stage_put(n).start()
            b_put(n, far, 1, far).start()
            b_put(n, near, 0, near).start()

        @pl.when(inner)
        def _():
            b_put(n, mir, 2, mir).start()
            b_put(n, near, 0, near).start()

    def combine(n):
        h, at, size = b_pc[n]

        @pl.when(inner)
        def _():
            stage_put(n).wait_recv()
            Pb[h, far, at:at + size] = Pb[h, far, at:at + size] + St[h, at:at + size]
            b_put(n, far, 1, far).start()

    def b_sum(n):
        h, at, size = b_pc[n]
        b_put(n, near, 0, near).wait_recv()
        part = Pb[h, z, at:at + size] + Rb[h, 0, at:at + size]

        @pl.when(inner)
        def _():
            b_put(n, mir, 2, mir).wait_recv()

        @pl.when(outer)
        def _():
            Rb[h, 2, at:at + size] = jnp.zeros((size, blk), F32)

        part = part + Rb[h, 2, at:at + size]
        b_put(n, far, 1, far).wait_recv()
        return part + Rb[h, 1, at:at + size]

    def pair_rhs(ref):
        hi, lo = split(ref.reshape(2 * blk, blk))
        return jnp.concatenate([hi, lo], axis=1)

    def pair_mm(ah, al, rhs):
        acc = mm(ah, rhs)
        return acc[:, :blk] + (acc[:, blk:] + mm(al, rhs[:, :blk]))

    def add_chip(h, chip, first=False):
        cols = pl.ds(pl.multiple_of(chip * (2 * blk), 2 * blk), 2 * blk)
        part = pair_mm(Ahi[:, cols], Alo[:, cols], pair_rhs(G[h, pl.ds(2 * chip, 2)])).reshape(reps, blk, blk)
        Pb[h] = part if first else Pb[h] + part

    for h in range(2):

        def forward(i, p):
            put(G.at[h, p], G.at[h, p], a_s.at[h, i], a_r.at[h, i], (p, z)).wait_recv()
            send(G.at[h, p], G.at[h, p], a_s.at[h, 3 + i], a_r.at[h, 3 + i], (sib, z))

        forward(1, xn)
        forward(2, yn)
        a_cp[h][3].wait_recv()
        add_chip(h, q, True)
        forward(3, dg)
        if h == 0:
            gather(1)
        else:
            combine(0)

        @pl.loop(1, 4)
        def _(i):
            p = row + (i % 2) * (2 - 4 * x) + (i // 2) * (4 - 8 * y)
            put(G.at[h, p], G.at[h, p], a_s.at[h, 3 + i], a_r.at[h, 3 + i], (sib, z)).wait_recv()
            add_chip(h, p // 2)

        for n in ((0,), (1, 2))[h]:
            b_send(n)

    @pl.loop(0, secs)
    def _(s):
        tt = [T[s, t].T for t in range(T.shape[1])]
        rows = pl.ds(pl.multiple_of(((s % 2) * chips + s // 2) * blk, blk), blk)
        for k in range(reps):
            m = masks(s, k)
            val = tt[0] * m[0]
            for t in range(1, T.shape[1]):
                val = val + tt[t] * m[t]
            hi, lo = split(val)
            AThi[rows, k * blk:(k + 1) * blk] = hi
            ATlo[rows, k * blk:(k + 1) * blk] = lo

    combine(1)
    combine(2)
    loads[3].wait()
    loads[4].wait()

    def d_put(n, k, slot, dev):
        h, at, size = d_pc[n]
        ref = Bk.at[h, k, at:at + size]
        return put(ref, ref, d_s.at[n, slot], d_r.at[n, slot], (row, dev))

    def d_send(n):
        d_put(n, z, 2, mir).start()

        @pl.when(outer)
        def _():
            d_put(n, z, 1, far).start()

        d_put(n, z, 0, near).start()

    w = W[...]
    agg0 = b_sum(0)
    pre0 = mm3(agg0, w[:blk])
    agg1, delta = [], []
    for n in (1, 2):
        at = b_pc[n][1]
        agg1.append(b_sum(n))
        pre = pre0[at:at + rh] + mm3(agg1[-1], w[blk:])
        sig = 1.0 / (1.0 + jnp.exp(-pre))
        delta.append(C[at:at + rh] * (sig * (1.0 + pre * (1.0 - sig))))
        back = mm3(delta[-1], w, ((1,), (1,)))
        for h in range(2):
            Bk[h, z, at:at + rh] = back[:, h * blk:(h + 1) * blk]
        d_send(n - 1)
        Ho[at:at + rh] = pre * sig
    agg = jnp.concatenate([agg0, jnp.concatenate(agg1, axis=0)], axis=1)
    delta = jnp.concatenate(delta, axis=0)
    hid_cp = pltpu.make_async_copy(Ho, hid_o, loc_sem.at[5])
    hid_cp.start()

    def relay(n):
        @pl.when(inner)
        def _():
            d_put(n, mir, 2, mir).wait_recv()
            d_put(n, mir, 1, near).start()


    wt[...] = mm3(agg.T, delta) * (1.0 / math.sqrt(blk * secs * reps))
    half = wt.shape[0] // 2
    piece = half // chips
    sub = piece // reps
    oth = pl.multiple_of((1 - c) * half, half)
    own = pl.multiple_of(c * half, half)
    g1 = send(wt.at[pl.ds(oth, half)], ws, g_s.at[0], g_r.at[0], (sib, z))
    relay(0)
    relay(1)

    @pl.when(outer)
    def _():
        for n in (0, 1):
            d_put(n, near, 0, near).wait_recv()

    d_send(2)
    drain()
    for n in range(3):
        for i in range(3):
            b_put(n, z, i, near).wait_send()
    g1.wait_recv()
    wc[...] = wt[pl.ds(own, half)] + ws[...]
    g2 = [send(wc.at[pl.ds(pl.multiple_of((p // 2) * piece, piece), piece)], wr.at[i], g_s.at[1 + i], g_r.at[1 + i], (p, z))
          for i, p in enumerate(plane)]

    def rows_start(h):
        parts = ((0, 1 - c), (1, c))
        at = [pl.ds(pl.multiple_of(core * (chips * blk), chips * blk), chips * blk) for _, core in parts]

        def pair(k):
            cols = pl.ds(pl.multiple_of(k * blk, 2 * blk), 2 * blk)
            rhs = pair_rhs(Bk[h, pl.ds(k, 2)])
            return [lambda a=a: pair_mm(AThi[a, cols], ATlo[a, cols], rhs).reshape(chips, blk, blk) for a in at]

        pieces = ((0, 1), (2,))[h]
        if h == 0:
            @pl.when(inner)
            def _():
                for n in pieces:
                    d_put(n, near, 0, near).wait_recv()
        else:
            for n in pieces:
                d_put(n, near, 0, near).wait_recv()
        here = (z // 2) * 2
        for i, part in enumerate(pair(here)):
            Rs[h, i] = part()
        for n in pieces:
            d_put(n, far, 1, far).wait_recv()

        @pl.when(outer)
        def _():
            for n in pieces:
                d_put(n, mir, 2, mir).wait_recv()

        out = []
        for i, part in enumerate(pair(2 - here)):
            Rs[h, i] = Rs[h, i] + part()
            if i == 0:
                out = [send(Rs.at[h, 0, p // 2], Es.at[h, p // 2], e_s.at[h, 3 + m], e_r.at[h, 3 + m], (sib, z))
                       for m, p in enumerate((dg, xn, yn, row))]
        return out

    def rows_mid(h, cps):
        out = []
        for i, p in enumerate((dg, xn, yn)):
            cps[i].wait_recv()
            Ec[h, i] = Rs[h, 1, p // 2] + Es[h, p // 2]
            out.append(send(Ec.at[h, i], Er.at[h, i], e_s.at[h, i], e_r.at[h, i], (p, z)))
        cps[3].wait_recv()
        return out

    def rows_end(h, cps):
        total = Rs[h, 1, q] + Es[h, q]
        for i, cp in enumerate(cps):
            cp.wait_recv()
            total = total + Er[h, i]
        Fo[:, h * blk:(h + 1) * blk] = total

    e0 = rows_start(0)
    relay(2)
    e0 = rows_mid(0, e0)

    at = pl.multiple_of(q * piece, piece)
    total = wc[pl.ds(at, piece)]
    for i in range(3):
        g2[i].wait_recv()
        total = total + wr[i]
    wz[...] = total
    g3 = [send(wz.at[pl.ds(pl.multiple_of(k * sub, sub), sub)], wzr.at[i], g_s.at[4 + i], g_r.at[4 + i], (row, k))
          for i, k in enumerate(zs)]

    total = wz[pl.ds(pl.multiple_of(z * sub, sub), sub)]
    for i in range(reps - 1):
        g3[i].wait_recv()
        total = total + wzr[i]
    top = c * half + q * piece
    mine = pl.ds(pl.multiple_of(top + z * sub, sub), sub)
    gw[mine] = total
    g4 = [send(gw.at[mine], gw.at[mine], g_s.at[7 + i], g_r.at[7 + i], (row, k)) for i, k in enumerate(zs)]
    e1 = rows_start(1)
    for cp in g4:
        cp.wait_recv()
    mine = pl.ds(pl.multiple_of(top, piece), piece)
    g5 = [send(gw.at[mine], gw.at[mine], g_s.at[10 + i], g_r.at[10 + i], (p, z)) for i, p in enumerate(plane)]

    e1 = rows_mid(1, e1)
    rows_end(0, e0)

    for cp in g5:
        cp.wait_recv()
    mine = pl.ds(own, half)
    g6 = send(gw.at[mine], gw.at[mine], g_s.at[13], g_r.at[13], (sib, z))

    rows_end(1, e1)
    f_cp = pltpu.make_async_copy(Fo, gf_o, loc_sem.at[6])
    f_cp.start()
    g6.wait_recv()
    g_cp = pltpu.make_async_copy(gw, gw_o, loc_sem.at[7])
    g_cp.start()
    drain()
    for n in range(3):
        for i in range(3):
            d_put(n, z, i, near).wait_send()
    hid_cp.wait()
    f_cp.wait()
    g_cp.wait()


def store(a, b, c, x, y, z, u, v, w, sem):
    bufs = ((a, u, x), (b, v, y), (c, w, z))
    ins = [pltpu.make_async_copy(s, t, sem.at[0, i]) for i, (s, t, _) in enumerate(bufs)]
    outs = [pltpu.make_async_copy(t, d, sem.at[1, i]) for i, (_, t, d) in enumerate(bufs)]
    for cp in ins:
        cp.start()
    for cp, out in zip(ins, outs):
        cp.wait()
        out.start()
    for out in outs:
        out.wait()


def fused(features, weight, cotangent, tiles, tile_count, tile_block):
    blk, width = features.shape
    secs, slots = tiles.shape[2], tiles.shape[3]
    reps = lax.axis_size("rep")
    chips = secs // 2
    half = width // 2
    piece = half // chips
    sub = piece // reps
    V = pltpu.VMEM
    dma = pltpu.SemaphoreType.DMA
    hbm = pl.BlockSpec(memory_space=pltpu.HBM)
    smem = pl.BlockSpec(memory_space=pltpu.SMEM)
    flops = 2 * 3 * 2 * (reps * blk) * (secs * blk) * width
    raw = pl.pallas_call(
        kernel,
        out_shape=(jax.ShapeDtypeStruct((blk, width), F32), jax.ShapeDtypeStruct((width, width), F32),
                   jax.ShapeDtypeStruct((blk, width), F32)),
        in_specs=[hbm, hbm, hbm, hbm, smem, smem],
        out_specs=(hbm,) * 3,
        scratch_shapes=[
            V((2, secs, blk, blk), F32), V((secs, slots, blk, blk), F32), V((width, width), F32), V((blk, width), F32),
            V((reps * blk, secs * blk), BF16), V((reps * blk, secs * blk), BF16),
            V((secs * blk, reps * blk), BF16), V((secs * blk, reps * blk), BF16),
            V((2, reps, blk, blk), F32), V((2, reps - 1, blk, blk), F32), V((2, blk, blk), F32), V((2, reps, blk, blk), F32),
            V((2, 2, chips, blk, blk), F32), V((2, chips, blk, blk), F32), V((2, 3, blk, blk), F32), V((2, 3, blk, blk), F32),
            V((blk, width), F32), V((blk, width), F32),
            V((width, width), F32), V((half, width), F32), V((half, width), F32), V((3, piece, width), F32),
            V((piece, width), F32), V((reps - 1, sub, width), F32), V((width, width), F32),
            dma((8,)), dma((2, 7)), dma((2, 7)), dma((3, 3)), dma((3, 3)), dma((3,)), dma((3, 3)), dma((3, 3)),
            dma((2, 7)), dma((2, 7)), dma((14,)), dma((14,)),
        ],
        compiler_params=pltpu.CompilerParams(collective_id=0, has_side_effects=True, vmem_limit_bytes=LIMIT),
        cost_estimate=pl.CostEstimate(flops=flops, bytes_accessed=4 * tiles.size, transcendentals=blk * width),
        name="graph_step",
    )(features, weight, cotangent, tiles, tile_count, tile_block.transpose(0, 1, 3, 2))
    return pl.pallas_call(
        store,
        out_shape=tuple(jax.ShapeDtypeStruct(r.shape, r.dtype) for r in raw),
        in_specs=[hbm] * 3,
        out_specs=(hbm,) * 3,
        scratch_shapes=[V(r.shape, r.dtype) for r in raw] + [dma((2, 3))],
        compiler_params=pltpu.CompilerParams(vmem_limit_bytes=LIMIT),
        name="store_results",
    )(*raw)


def silu_slope(pre):
    sig = jax.nn.sigmoid(pre)
    return sig * (1.0 + pre * (1.0 - sig))


def body(features, weight, cotangent, tiles, tile_count, tile_block):
    highest = lax.Precision.HIGHEST
    tile_set = tiles[0, 0]
    counts = tile_count[0, 0]
    block_ids = tile_block[0, 0]
    sections = tile_set.shape[0]
    slots = tile_set.shape[1]
    blk = tile_set.shape[2]
    width = features.shape[1]
    groups = lax.axis_size("rep")
    select = (
        (block_ids[..., None] == jnp.arange(groups, dtype=jnp.int32))
        & (jnp.arange(slots, dtype=jnp.int32)[:, None] < counts[:, None, None])
    ).astype(jnp.float32)
    gathered = lax.all_gather(features, "rows", axis=0, tiled=True).reshape(sections, blk, width)
    prods = jnp.einsum("stab,sbf->staf", tile_set, gathered, precision=highest)
    total = jnp.einsum("stk,staf->kaf", select, prods, precision=highest)
    aggregated = lax.psum_scatter(
        total.reshape(groups * blk, width), "rep", scatter_dimension=0, tiled=True
    )
    pre = jnp.dot(aggregated, weight, precision=highest)
    hidden = jax.nn.silu(pre)
    delta = cotangent * silu_slope(pre)
    weight_term = jnp.dot(aggregated.T, delta, precision=highest)
    node_total = blk * lax.axis_size("rows") * groups
    grad_weight = lax.psum(weight_term, ("rows", "rep")) / math.sqrt(node_total)
    back = jnp.dot(delta, weight.T, precision=highest)
    group_back = lax.all_gather(back, "rep", axis=0, tiled=True).reshape(groups, blk, width)
    count = sections * blk
    picked = jnp.einsum("stk,kaf->staf", select, group_back, precision=highest)
    result = jnp.einsum("stab,staf->sbf", tile_set, picked, precision=highest)
    all_terms = result.reshape(count, width)
    grad_features = lax.psum_scatter(all_terms, "rows", scatter_dimension=0, tiled=True)
    return (hidden, grad_weight, grad_features)


def solution(mesh):
    in_specs = (
        P(("rows", "rep"), None),
        P(),
        P(("rows", "rep"), None),
        P("rows", "rep", None, None, None, None),
        P("rows", "rep", None),
        P("rows", "rep", None, None),
    )
    out_specs = (P(("rows", "rep"), None), P(), P(("rows", "rep"), None))
    fits = mesh.shape["rows"] == 8 and mesh.shape["rep"] == 4
    return jax.shard_map(fused if fits else body, mesh=mesh, in_specs=in_specs, out_specs=out_specs, check_vma=False)
```
